256 devices in a mesh: section: 2 (over core), wide: 16 (over x, z_lo), narrow: 8 (over y, z_hi).
Axes of the slice: x: 4, y: 4, z: 8 (z_hi: 2, z_lo: 4; z = z_hi * 4 + z_lo), core: 2. Of those that a mesh axis runs over, the one named last changes fastest.
Arguments:
- queries: bfloat16 [8, 1024, 8192], P('narrow', None, 'wide'), may hold values from -8 to 8
- keys_values: bfloat16 [8, 1024, 2048], P('narrow', None, 'wide'), may hold values from -6 to 6
- segments: int32 [8, 1024], P('narrow'), may hold values from 0 to 1016, as said below
- residual: bfloat16 [8, 1024, 8192], P('narrow', None, 'wide'), may hold values from -10 to 10
- out_weight: bfloat16 [8192, 8192], P('wide'), may hold values from -1 to 1
- key_weight: bfloat16 [8192, 512], P('wide'), may hold values from -0.0625 to 0.0625
- key_bias: float32 [512], replicated, may hold values from -4 to 4
- norm_gain: float32 [8192], P('wide'), may hold values from 0.5 to 1.5
Outputs:
- handed: bfloat16 [8, 1024, 8192], P('narrow', None, 'wide')
- keys_b: bfloat16 [8, 1024, 512], P('narrow', 'section')
The draws below stay inside these ranges and needn't reach their ends.
Inputs may be any that keep to these rules, and one draw needn't show every extreme that they name: segments[s, t] is 0 at t = 0, never falls, changes only at multiples of 8, equals t wherever it changes, and the last 8 positions of every sequence form a text of their own.
All inputs are finite; a program needn't handle non-finite values.
Results may differ from the reference program's by a relative error of at most 0.025.
Values may be sent and summed in bfloat16 or wider, within the bound.
A program may use at most 128 MiB of HBM per device.

```python
import math
import jax
import jax.numpy as jnp
from jax import lax

D = 8192
HEADS = 64
KV_HEADS = 8
HEAD = 128
KB_HEADS = 4
LEN = 1024
SEQS = 8
N_WIDE = 16


def draw_queries(key, part):
    key = jax.random.fold_in(key, 12)
    values = jnp.clip(jax.random.normal(key, (SEQS, LEN, HEADS, HEAD), jnp.float32), -6.0, 6.0)
    return values.reshape(SEQS, LEN, HEADS * HEAD).astype(jnp.bfloat16)


def draw_keys_values(key, part):
    key = jax.random.fold_in(key, 11)
    value_key, scale_key = jax.random.split(key)
    scales = jnp.power(10.0, jax.random.uniform(scale_key, (SEQS, LEN, 1, 1, 1), jnp.float32, -0.5, 0.5))
    values = jax.random.normal(value_key, (SEQS, LEN, KV_HEADS, 2, HEAD), jnp.float32)
    values = jnp.clip(values * scales, -6.0, 6.0)
    return values.reshape(SEQS, LEN, 2 * KV_HEADS * HEAD).astype(jnp.bfloat16)


def draw_segments(key, part):
    key = jax.random.fold_in(key, 13)
    blocks = LEN // 8
    opens = jax.random.randint(key, (SEQS, blocks), 0, 4) == 0
    index = jnp.arange(blocks, dtype=jnp.int32)
    opens = opens | (index == 0)[None, :] | (index == blocks - 1)[None, :]
    starts = lax.cummax(jnp.where(opens, index[None, :] * 8, 0), axis=1)
    return jnp.repeat(starts, 8, axis=1).astype(jnp.int32)


def draw_residual(key, part):
    key = jax.random.fold_in(key, 14)
    value_key, row_key, column_key = jax.random.split(key, 3)
    row_scales = jnp.power(10.0, jax.random.uniform(row_key, (SEQS, LEN, 1), jnp.float32, -0.5, 0.5))
    ramp = jnp.arange(D, dtype=jnp.float32) / (D - 1) - 0.5
    jitter = jax.random.uniform(column_key, (D,), jnp.float32, -0.15, 0.15)
    column_scales = jnp.power(10.0, ramp + jitter).reshape(1, 1, D)
    values = jnp.clip(0.2 * jax.random.normal(value_key, (SEQS, LEN, D), jnp.float32), -1.0, 1.0)
    return jnp.clip(values * row_scales * column_scales, -9.9, 9.9).astype(jnp.bfloat16)


def weight_columns(key, span):
    ramp = jnp.arange(D, dtype=jnp.float32) / (D - 1) - 0.5
    jitter = jax.random.uniform(key, (D,), jnp.float32, -0.1, 0.1)
    return jnp.power(10.0, span * ramp + jitter).reshape(1, D)


def draw_out_weight(key, part):
    key = jax.random.fold_in(key, 15)
    value_key, column_key = jax.random.split(key)
    fan_scale = (HEADS * HEAD // 8) ** (-0.5)
    values = jnp.clip(jax.random.normal(value_key, (HEADS * HEAD, D), jnp.float32), -6.0, 6.0)
    columns = weight_columns(column_key, 0.8)
    return jnp.clip(values * fan_scale * columns, -1.0, 1.0).astype(jnp.bfloat16)


def block_scale(rng, extent, pieces, low, largest):
    loudness = 1.0
    for dim, parts in pieces:
        heights = jax.random.uniform(jax.random.fold_in(jax.random.fold_in(rng, 6), dim), (parts,), jnp.float32, low / len(pieces), largest / len(pieces))
        loudness = loudness * jnp.repeat(jnp.exp(heights), extent[dim] // parts).reshape((-1,) + (1,) * (len(extent) - 1 - dim))
    return loudness


def centred(own_key, dims, deviation, most, pieces=(), kind=jnp.bfloat16):
    loudness = block_scale(own_key, dims, pieces, -0.22, 0.18) if pieces else 1.0
    result = jax.random.normal(own_key, dims, jnp.float32) * deviation * loudness
    return jnp.minimum(jnp.maximum(result, -most), most).astype(kind)


def setup_inputs(seed: int = 0) -> dict:
    key_of = jax.random.split(jax.random.key(seed), 9)
    return {
        "queries": draw_queries(jax.random.fold_in(key_of[8], 71), 0),
        "keys_values": draw_keys_values(jax.random.fold_in(key_of[8], 71), 0),
        "segments": draw_segments(jax.random.fold_in(key_of[8], 71), 0),
        "residual": draw_residual(jax.random.fold_in(key_of[8], 71), 0),
        "out_weight": draw_out_weight(jax.random.fold_in(key_of[8], 71), 0),
        "key_weight": centred(key_of[5], (D, KB_HEADS * HEAD), D ** -0.5, 0.0625, ((0, 16),)),
        "key_bias": centred(key_of[6], (KB_HEADS * HEAD,), 1.0, 4.0, (), jnp.float32),
        "norm_gain": jnp.clip(1.0 + 0.1 * jax.random.normal(key_of[7], (D,), jnp.float32), 0.5, 1.5),
    }


theta = 1000000.0
eps = 1e-06
masked = -1e+30

def rotate(vectors, positions):
    half = HEAD // 2
    freq = jnp.power(theta, -2.0 * jnp.arange(half, dtype=jnp.float32) / HEAD)
    angles = positions.astype(jnp.float32)[:, None] * freq[None, :]
    cosine = jnp.cos(angles)[:, None, :]
    sine = jnp.sin(angles)[:, None, :]
    leading = vectors[..., :half]
    trailing = vectors[..., half:]
    return jnp.concatenate([leading * cosine - trailing * sine, trailing * cosine + leading * sine], axis=-1)

def attend_group(grouped, paired, segments):
    scale = 1.0 / math.sqrt(HEAD)
    scores = jnp.einsum('qhd,kd->hqk', grouped.astype(jnp.float32), paired[:, 0].astype(jnp.float32)) * scale
    positions = jnp.arange(LEN, dtype=jnp.int32)
    allowed = (segments[:, None] == segments[None, :]) & (positions[:, None] >= positions[None, :])
    scores = jnp.where(allowed[None], scores, masked)
    weights = jnp.exp(scores - lax.optimization_barrier(jnp.max(scores, axis=-1, keepdims=True)))
    probs = (weights / lax.optimization_barrier(jnp.sum(weights, axis=-1, keepdims=True))).astype(jnp.bfloat16)
    probs = lax.optimization_barrier(probs)
    context = jnp.einsum('hqk,kd->qhd', probs.astype(jnp.float32), paired[:, 1].astype(jnp.float32))
    return context.astype(jnp.bfloat16).reshape(LEN, -1)

def one_sequence(items, out_weight, key_weight, key_bias, norm_gain):
    queries, pairs, segments, residual = items
    grouped = queries.reshape(LEN, KV_HEADS, HEADS // KV_HEADS, HEAD).transpose(1, 0, 2, 3)
    paired = pairs.reshape(LEN, KV_HEADS, 2, HEAD).transpose(1, 0, 2, 3)
    context = lax.map(lambda item: attend_group(item[0], item[1], segments), (grouped, paired))
    context = context.transpose(1, 0, 2).reshape(LEN, HEADS * HEAD)
    width = HEADS * HEAD // N_WIDE

    def add_part(index, total):
        offset = (jnp.asarray(index, jnp.int32) * width).astype(jnp.int32)
        columns = lax.dynamic_slice_in_dim(context, offset, width, 1)
        weights = lax.dynamic_slice_in_dim(out_weight, offset, width, 0)
        part = jnp.dot(columns, weights, preferred_element_type=jnp.float32).astype(jnp.bfloat16)
        part = lax.optimization_barrier(part)
        return total + part.astype(jnp.float32)
    summed = lax.fori_loop(0, N_WIDE, add_part, jnp.zeros((LEN, D), jnp.float32))
    handed = (residual.astype(jnp.float32) + summed).astype(jnp.bfloat16)
    hidden = handed.astype(jnp.float32)
    inverse = lax.rsqrt(lax.optimization_barrier(jnp.mean(hidden * hidden, axis=-1, keepdims=True)) + eps)
    normed = (hidden * inverse * norm_gain).astype(jnp.bfloat16)
    projected = jnp.dot(normed, key_weight, preferred_element_type=jnp.float32) + key_bias
    rotated = rotate(projected.reshape(LEN, KB_HEADS, HEAD), jnp.arange(LEN, dtype=jnp.int32))
    return (handed, rotated.reshape(LEN, KB_HEADS * HEAD).astype(jnp.bfloat16))

def reference(queries, keys_values, segments, residual, out_weight, key_weight, key_bias, norm_gain):
    handed, keys_b = lax.map(lambda items: one_sequence(items, out_weight, key_weight, key_bias, norm_gain), (queries, keys_values, segments, residual))
    return (handed, keys_b)
```

```python
import functools
import math

import jax
import jax.numpy as jnp
import numpy as np
from jax import lax
from jax.experimental import pallas as pl
from jax.experimental.pallas import tpu as pltpu
from jax.sharding import PartitionSpec as P

MESH = pl.DeviceIdType.MESH
D = 8192
HEAD = 128
LEN = 1024
HALF = LEN // 2
COLS = 512
KEYS = 512
THETA = 1000000.0
EPS = 1e-06
MASKED = -1e30
SCALE = math.log2(math.e) / math.sqrt(HEAD)
BF16 = jnp.bfloat16
F32 = jnp.float32
WIDE_KEYS = KEYS + 128


def dot(a, b, dims=((1,), (0,))):
    return lax.dot_general(a, b, (dims, ((), ())), preferred_element_type=F32)


def split_sum(total):
    rows = total.shape[0]
    high = total.astype(BF16).astype(F32)
    low = total - high
    lane = lax.broadcasted_iota(jnp.int32, (rows, 128), 1)
    return jnp.where(lane < 64, high, low).astype(BF16)


def kernel(
    q_hbm, kv_hbm, seg_ref, res_hbm, w_hbm, kw_hbm, bias_ref, gain_ref, rot_hbm,
    hand_hbm, keys_hbm,
    qbuf, kvb, wbuf, resb, kwb, rotb, cbuf, pbuf, xsend, xrecv, zsend, zrecv, hbuf,
    k1s, k1r, k2s, k2r, k3,
    l_sem, wl_sem, kv_sem, wx_sem, wy_sem, c_sem, p_sem, zs_sem, zr_sem, h_sem, hl_sem,
    ks_sem, kr_sem, kl_sem,
):
    c = lax.axis_index("section")
    w = lax.axis_index("wide")
    n = lax.axis_index("narrow")
    x, z = w // 4, w % 4
    y, h = n // 2, n % 2

    def at(c_=None, x_=None, y_=None, z_=None):
        xx = x if x_ is None else x_
        zz = z if z_ is None else z_
        yy = y if y_ is None else y_
        return {"section": c if c_ is None else c_, "wide": xx * 4 + zz, "narrow": yy * 2 + h}

    def plus(value, by):
        return (value + by) % 4

    started = []

    def send(src, dst, send_sem, recv_sem, to):
        copy = pltpu.make_async_remote_copy(
            src_ref=src, dst_ref=dst, send_sem=send_sem, recv_sem=recv_sem,
            device_id=to, device_id_type=MESH,
        )
        copy.start()
        started.append(copy)

    def arrived(dst, recv_sem):
        pltpu.make_async_remote_copy(
            src_ref=dst, dst_ref=dst, send_sem=recv_sem, recv_sem=recv_sem,
            device_id=at(1 - c), device_id_type=MESH,
        ).wait_recv()

    owner = [3 * (1 - z // 2), (2 + 3 * z) % 5, 1 + z % 2, z]
    pair = z + 1 - 2 * (z % 2)
    mine = z % 2
    rows = pl.ds(pl.multiple_of(c * HALF, HALF), HALF)

    heads = pl.ds(pl.multiple_of(c * 256, 256), 256)
    local_kv = pltpu.make_async_copy(kv_hbm, kvb.at[mine], l_sem.at[0])
    local_q = pltpu.make_async_copy(q_hbm.at[:, heads], qbuf, l_sem.at[1])
    local_res = pltpu.make_async_copy(res_hbm.at[rows], resb, l_sem.at[2])
    local_kw = pltpu.make_async_copy(kw_hbm, kwb, l_sem.at[3])
    local_rot = [
        pltpu.make_async_copy(
            rot_hbm.at[:, pl.ds(pl.multiple_of(c * HALF + 256 * g + 64 * x + 16 * z, 16), 16)],
            rotb.at[g], l_sem.at[4 + g],
        )
        for g in range(2)
    ]

    def columns(k, x_):
        return pl.ds(pl.multiple_of(x_ * (4 * COLS) + owner[k] * COLS, COLS), COLS)

    local_w = [
        pltpu.make_async_copy(w_hbm.at[heads, columns(k, x)], wbuf.at[k, 0], wl_sem.at[k])
        for k in range(4)
    ]
    for copy in [local_kv, local_q, *local_w, local_res, local_kw, *local_rot]:
        copy.start()

    barrier = pltpu.get_barrier_semaphore()
    partners = [at(1 - c)]
    for d in range(1, 4):
        partners += [at(x_=plus(x, d)), at(y_=plus(y, d)), at(z_=plus(z, d))]
    for to in partners:
        pl.semaphore_signal(barrier, inc=1, device_id=to, device_id_type=MESH)
    pl.semaphore_wait(barrier, len(partners))

    send(kv_hbm.at[rows], kvb.at[mine, rows], kv_sem.at[0], kv_sem.at[1], at(z_=pair))
    part = pl.ds(pl.multiple_of(y * 64, 64), 64)
    w_rows = pl.ds(pl.multiple_of(c * 256 + y * 64, 64), 64)
    for k in range(4):
        for d in range(1, 4):
            to = plus(x, 4 - d)
            send(w_hbm.at[w_rows, columns(k, to)], wbuf.at[k, d, part],
                 wx_sem.at[0, k, d], wx_sem.at[1, k, d], at(x_=to))

    def share_weights(k):
        for d in range(1, 4):
            arrived(wbuf.at[k, d, part], wx_sem.at[1, k, d])
        for e in range(1, 4):
            send(wbuf.at[k, pl.ds(1, 3), part], wbuf.at[k, pl.ds(1, 3), part],
                 wy_sem.at[0, k, e], wy_sem.at[1, k, e], at(y_=plus(y, e)))

    def await_weights(k):
        local_w[k].wait()
        for e in range(1, 4):
            theirs = pl.ds(pl.multiple_of(plus(y, 4 - e) * 64, 64), 64)
            arrived(wbuf.at[k, pl.ds(1, 3), theirs], wy_sem.at[1, k, e])

    local_kv.wait()
    local_q.wait()
    arrived(kvb.at[1 - mine, rows], kv_sem.at[1])
    send(kvb.at[1 - mine, rows], kvb.at[1 - mine, rows], kv_sem.at[2], kv_sem.at[3], at(1 - c))
    share_weights(0)
    other_rows = pl.ds(pl.multiple_of((1 - c) * HALF, HALF), HALF)
    arrived(kvb.at[1 - mine, other_rows], kv_sem.at[3])

    def attend(index):
        seen = 128 * (index + 1)
        here = pl.ds(128 * index, 128)
        picked = jnp.concatenate([qbuf[here, :HEAD], qbuf[here, HEAD:]], axis=0)
        scores = dot(kvb[0, :seen, :], picked, ((1,), (1,)))
        first = seg_ref[:, here]
        first = jnp.concatenate([first, first], axis=1)
        key_at = lax.broadcasted_iota(jnp.int32, (seen, 256), 0)
        query_at = 128 * index + lax.broadcasted_iota(jnp.int32, (seen, 256), 1) % 128
        scores = jnp.where((key_at >= first) & (key_at <= query_at), scores, MASKED)
        top = jnp.max(scores, axis=0, keepdims=True)
        weights = jnp.exp2((scores - top) * SCALE)
        total = jnp.sum(weights, axis=0, keepdims=True)
        context = dot(kvb[1, :seen, :], weights.astype(BF16), ((0,), (0,)))
        return (context / total).T.astype(BF16)

    def context_block(b):
        for half in range(2):
            context = attend(b + 4 * half)
            there = pl.ds(128 * half, 128)
            cbuf[0, b, there, :HEAD] = context[:128]
            cbuf[0, b, there, HEAD:] = context[128:]
        for d in range(1, 4):
            send(cbuf.at[0, b], cbuf.at[d, b], c_sem.at[0, b, d], c_sem.at[1, b, d],
                 at(x_=plus(x, 4 - d)))

    for b in range(4):
        context_block(b)
        if b < 3:
            share_weights(b + 1)

    units = [(k, 2 * g + j) for g in range(2) for k in range(4) for j in range(2)]
    met_k, met_b = set(), set()

    def multiply(u):
        k, b = units[u]
        if k not in met_k:
            met_k.add(k)
            await_weights(k)
        if b not in met_b:
            met_b.add(b)
            for d in range(1, 4):
                arrived(cbuf.at[d, b], c_sem.at[1, b, d])
        total = dot(cbuf[0, b], wbuf[k, 0])
        for d in range(1, 4):
            total += dot(cbuf[d, b], wbuf[k, d])
        slot = u % 2
        pbuf[slot, 0] = total[:128]
        pbuf[slot, 1] = total[128:]
        xsend[u] = pbuf[slot, 1 - c].astype(BF16)
        send(xsend.at[u], xrecv.at[u], p_sem.at[0, u], p_sem.at[1, u], at(1 - c))

    def pass_on(u):
        k, b = units[u]
        arrived(xrecv.at[u], p_sem.at[1, u])
        total = pbuf[u % 2, c] + xrecv[u].astype(F32)
        if k < 3:
            to = owner[k]
            up = to > z
            has = (up & (z > 0)) | (jnp.logical_not(up) & (z < 3))

            @pl.when(has)
            def _():
                arrived(zrecv.at[to, b], zr_sem.at[to, b])
                zsend[k, b] = (total + zrecv[to, b].astype(F32)).astype(BF16)

            @pl.when(jnp.logical_not(has))
            def _():
                zsend[k, b] = total.astype(BF16)

            following = jnp.where(up, z + 1, z - 1)
            slot = jnp.where(jnp.logical_not(up) & (to == following), 4, to)
            send(zsend.at[k, b], zrecv.at[slot, b], zs_sem.at[k, b], zr_sem.at[slot, b],
                 at(z_=following))
        else:
            pbuf[u % 2, c] = total + resb[pl.ds(128 * b, 128), :].astype(F32)

            @pl.when(z > 0)
            def _():
                arrived(zrecv.at[z, b], zr_sem.at[z, b])
                pbuf[u % 2, c] += zrecv[z, b].astype(F32)

            @pl.when(z < 3)
            def _():
                arrived(zrecv.at[4, b], zr_sem.at[4, b])
                pbuf[u % 2, c] += zrecv[4, b].astype(F32)

            hbuf[b] = pbuf[u % 2, c].astype(BF16)
            place = pl.ds(pl.multiple_of(c * HALF + 128 * b, 128), 128)
            local = pltpu.make_async_copy(hbuf.at[b], hand_hbm.at[place], hl_sem.at[b])
            local.start()
            locals_.append(local)
            send(hbuf.at[b], hand_hbm.at[place], h_sem.at[0, b], h_sem.at[1, b], at(1 - c))

    locals_ = []

    def keys_1(g):
        hidden = hbuf[pl.ds(2 * g, 2)].reshape(256, COLS).astype(F32)
        squares = jnp.sum(hidden * hidden, axis=1, keepdims=True)
        partial = dot((hidden * gain_ref[...]).astype(BF16), kwb[...])
        k1s[g, :, :KEYS] = partial.astype(BF16)
        k1s[g, :, KEYS:] = split_sum(squares)
        for d in range(1, 4):
            to = plus(x, 4 - d)
            send(k1s.at[g, pl.ds(pl.multiple_of(to * 64, 64), 64)], k1r.at[g, d],
                 ks_sem.at[0, g, d], kr_sem.at[0, g, d], at(x_=to))

    def keys_2(g):
        total = k1s[g, pl.ds(pl.multiple_of(x * 64, 64), 64), :].astype(F32)
        for d in range(1, 4):
            arrived(k1r.at[g, d], kr_sem.at[0, g, d])
            total += k1r[g, d].astype(F32)
        squares = total[:, KEYS : KEYS + 1] + total[:, KEYS + 64 : KEYS + 65]
        k2s[g, :, :KEYS] = total[:, :KEYS].astype(BF16)
        k2s[g, :, KEYS:] = split_sum(squares)
        for e in range(1, 4):
            to = plus(z, e)
            send(k2s.at[g, pl.ds(pl.multiple_of(to * 16, 16), 16)], k2r.at[g, e],
                 ks_sem.at[1, g, e], kr_sem.at[1, g, e], at(z_=to))

    def keys_3(g):
        at_rows = pl.ds(pl.multiple_of(z * 16, 16), 16)
        total = k2s[g, at_rows, :].astype(F32)
        for e in range(1, 4):
            arrived(k2r.at[g, e], kr_sem.at[1, g, e])
            total += k2r[g, e].astype(F32)
        squares = total[:, KEYS : KEYS + 1] + total[:, KEYS + 64 : KEYS + 65]
        projected = total[:, :KEYS] * lax.rsqrt(squares / D + EPS) + bias_ref[...]
        cosine, sine = rotb[g, 0], rotb[g, 1]
        for head in range(KEYS // HEAD):
            v = projected[:, head * HEAD : (head + 1) * HEAD]
            crossed = jnp.concatenate([v[:, HEAD // 2 :], v[:, : HEAD // 2]], axis=1)
            k3[g, at_rows, head * HEAD : (head + 1) * HEAD] = (v * cosine + crossed * sine).astype(BF16)
        for e in range(1, 4):
            send(k3.at[g, at_rows], k3.at[g, at_rows], ks_sem.at[2, g, e], kr_sem.at[2, g, e],
                 at(z_=plus(z, e)))

    def keys_4(g):
        for e in range(1, 4):
            theirs = pl.ds(pl.multiple_of(plus(z, 4 - e) * 16, 16), 16)
            arrived(k3.at[g, theirs], kr_sem.at[2, g, e])
        place = pl.ds(pl.multiple_of(256 * g + x * 64, 64), 64)
        local = pltpu.make_async_copy(k3.at[g], keys_hbm.at[place], kl_sem.at[g])
        local.start()
        locals_.append(local)
        for d in range(1, 4):
            send(k3.at[g], keys_hbm.at[place], ks_sem.at[3, g, d], kr_sem.at[3, g, d],
                 at(x_=plus(x, d)))

    local_res.wait()
    local_kw.wait()
    for copy in local_rot:
        copy.wait()
    last = len(units) - 1
    for u in range(last + 2):
        if u <= last:
            multiply(u)
        if u >= 1:
            pass_on(u - 1)
        if u == 8:
            keys_1(0)
        if u == 10:
            keys_2(0)
        if u == 12:
            keys_3(0)
        if u == 14:
            keys_4(0)
    keys_1(1)
    keys_2(1)
    keys_3(1)
    keys_4(1)
    for b in range(4):
        place = pl.ds(pl.multiple_of((1 - c) * HALF + 128 * b, 128), 128)
        arrived(hand_hbm.at[place], h_sem.at[1, b])
    for g in range(2):
        for d in range(1, 4):
            place = pl.ds(pl.multiple_of(256 * g + plus(x, 4 - d) * 64, 64), 64)
            arrived(keys_hbm.at[place], kr_sem.at[3, g, d])
    for copy in locals_:
        copy.wait()
    for copy in started:
        copy.wait_send()


def rotation():
    angles = np.arange(LEN)[:, None] * THETA ** (-2.0 * np.arange(HEAD // 2) / HEAD)[None, :]
    cosine, sine = np.cos(angles), np.sin(angles)
    return np.stack(
        [np.concatenate([cosine, cosine], 1), np.concatenate([-sine, sine], 1)]
    ).astype(np.float32)


def local(queries, keys_values, segments, residual, out_weight, key_weight, key_bias, norm_gain):
    hbm = pl.BlockSpec(memory_space=pl.ANY)
    vmem = pl.BlockSpec(memory_space=pltpu.VMEM)
    dma = pltpu.SemaphoreType.DMA
    handed, keys = pl.pallas_call(
        kernel,
        out_shape=(
            jax.ShapeDtypeStruct((LEN, COLS), BF16),
            jax.ShapeDtypeStruct((HALF, KEYS), BF16),
        ),
        in_specs=[hbm, hbm, vmem, hbm, hbm, hbm, vmem, vmem, hbm],
        out_specs=(hbm, hbm),
        scratch_shapes=[
            pltpu.VMEM((LEN, 256), BF16),
            pltpu.VMEM((2, LEN, HEAD), BF16),
            pltpu.VMEM((4, 4, 256, COLS), BF16),
            pltpu.VMEM((HALF, COLS), BF16),
            pltpu.VMEM((COLS, KEYS), BF16),
            pltpu.VMEM((2, 2, 16, HEAD), F32),
            pltpu.VMEM((4, 4, 256, 256), BF16),
            pltpu.VMEM((2, 2, 128, COLS), F32),
            pltpu.VMEM((16, 128, COLS), BF16),
            pltpu.VMEM((16, 128, COLS), BF16),
            pltpu.VMEM((3, 4, 128, COLS), BF16),
            pltpu.VMEM((5, 4, 128, COLS), BF16),
            pltpu.VMEM((4, 128, COLS), BF16),
            pltpu.VMEM((2, 256, WIDE_KEYS), BF16),
            pltpu.VMEM((2, 4, 64, WIDE_KEYS), BF16),
            pltpu.VMEM((2, 64, WIDE_KEYS), BF16),
            pltpu.VMEM((2, 4, 16, WIDE_KEYS), BF16),
            pltpu.VMEM((2, 64, KEYS), BF16),
            dma((6,)),
            dma((4,)),
            dma((4,)),
            dma((2, 4, 4)),
            dma((2, 4, 4)),
            dma((2, 4, 4)),
            dma((2, 16)),
            dma((3, 4)),
            dma((5, 4)),
            dma((2, 4)),
            dma((4,)),
            dma((4, 2, 4)),
            dma((4, 2, 4)),
            dma((2,)),
        ],
        compiler_params=pltpu.CompilerParams(
            collective_id=0, has_side_effects=True, vmem_limit_bytes=56 << 20
        ),
        name="relay",
    )(
        queries[0], keys_values[0], segments, residual[0], out_weight, key_weight,
        key_bias.reshape(1, KEYS), norm_gain.reshape(1, COLS), jnp.asarray(rotation()),
    )
    return handed[None], keys[None]


def solution(mesh):
    return jax.shard_map(
        local,
        mesh=mesh,
        in_specs=(
            P("narrow", None, "wide"),
            P("narrow", None, "wide"),
            P("narrow", None),
            P("narrow", None, "wide"),
            P("wide", None),
            P("wide", None),
            P(),
            P("wide"),
        ),
        out_specs=(P("narrow", None, "wide"), P("narrow", "section", None)),
        check_vma=False,
    )
```

```python
import functools
import math

import jax
import jax.numpy as jnp
import numpy as np
from jax import lax
from jax.experimental import pallas as pl
from jax.experimental.pallas import tpu as pltpu
from jax.sharding import PartitionSpec as P

MESH = pl.DeviceIdType.MESH
D = 8192
HEAD = 128
LEN = 1024
HALF = LEN // 2
COLS = 512
KEYS = 512
THETA = 1000000.0
EPS = 1e-06
MASKED = -1e30
SCALE = math.log2(math.e) / math.sqrt(HEAD)
BF16 = jnp.bfloat16
F32 = jnp.float32
GROUP = 256
UNITS = [(k, b) for k in range(4) for b in range(4)]


def dot(a, b, dims=((1,), (0,))):
    return lax.dot_general(a, b, (dims, ((), ())), preferred_element_type=F32)


def kernel(
    q_hbm, kv_hbm, seg_ref, res_hbm, w_hbm, kw_hbm, gain_ref,
    hand_hbm, keys_hbm, squares_ref,
    qbuf, kvb, wbuf, resb, kwb, gkb, cbuf, pbuf, xsend, xrecv, zsend, zrecv, hbuf,
    k1s, k1r, k2s, k2r, k3, sq1, sq2,
    l_sem, wl_sem, kv_sem, wx_sem, wy_sem, c_sem, p_sem, zs_sem, zr_sem, h_sem, hl_sem,
    gs_sem, gr_sem, ks_sem, kr_sem, kl_sem, qs_sem, qr_sem,
):
    c = lax.axis_index("section")
    w = lax.axis_index("wide")
    n = lax.axis_index("narrow")
    x, z = w // 4, w % 4
    y, h = n // 2, n % 2

    def at(c_=None, x_=None, y_=None, z_=None):
        xx = x if x_ is None else x_
        zz = z if z_ is None else z_
        yy = y if y_ is None else y_
        return {"section": c if c_ is None else c_, "wide": xx * 4 + zz, "narrow": yy * 2 + h}

    def plus(value, by):
        return (value + by) % 4

    started = []

    def send(src, dst, send_sem, recv_sem, to):
        copy = pltpu.make_async_remote_copy(
            src_ref=src, dst_ref=dst, send_sem=send_sem, recv_sem=recv_sem,
            device_id=to, device_id_type=MESH,
        )
        copy.start()
        started.append(copy)

    def arrived(dst, recv_sem):
        pltpu.make_async_remote_copy(
            src_ref=dst, dst_ref=dst, send_sem=recv_sem, recv_sem=recv_sem,
            device_id=at(1 - c), device_id_type=MESH,
        ).wait_recv()

    barrier = pltpu.get_barrier_semaphore()
    partners = [at(1 - c)]
    for d in range(1, 4):
        partners += [at(x_=plus(x, d)), at(y_=plus(y, d)), at(z_=plus(z, d))]
    for to in partners:
        pl.semaphore_signal(barrier, inc=1, device_id=to, device_id_type=MESH)

    owner = [3 * (1 - z // 2), (2 + 3 * z) % 5, 1 + z % 2, z]
    pair = z + 1 - 2 * (z % 2)
    mine = z % 2
    rows = pl.ds(pl.multiple_of(c * HALF, HALF), HALF)

    heads = pl.ds(pl.multiple_of(c * 256, 256), 256)
    local_kv = pltpu.make_async_copy(kv_hbm, kvb.at[mine], l_sem.at[0])
    local_q = pltpu.make_async_copy(q_hbm.at[:, heads], qbuf, l_sem.at[1])
    local_res = pltpu.make_async_copy(res_hbm.at[rows], resb, l_sem.at[2])
    local_kw = pltpu.make_async_copy(kw_hbm, kwb, l_sem.at[3])
    def columns(k, x_):
        return pl.ds(pl.multiple_of(x_ * (4 * COLS) + owner[k] * COLS, COLS), COLS)

    local_w = [
        pltpu.make_async_copy(w_hbm.at[heads, columns(k, x)], wbuf.at[k, 0], wl_sem.at[k])
        for k in range(4)
    ]
    for copy in [local_kv, local_kw, local_q, *local_w, local_res]:
        copy.start()

    pl.semaphore_wait(barrier, len(partners))

    send(kv_hbm.at[rows], kvb.at[mine, rows], kv_sem.at[0], kv_sem.at[1], at(z_=pair))
    part = pl.ds(pl.multiple_of(y * 64, 64), 64)
    w_rows = pl.ds(pl.multiple_of(c * 256 + y * 64, 64), 64)

    def send_weights(k):
        for d in range(1, 4):
            to = plus(x, 4 - d)
            send(w_hbm.at[w_rows, columns(k, to)], wbuf.at[k, d, part],
                 wx_sem.at[0, k, d], wx_sem.at[1, k, d], at(x_=to))

    def weights(i, e):
        theirs = pl.ds(pl.multiple_of(plus(y, 4 - e) * 64, 64), 64)
        return wbuf.at[i // 2, pl.ds(1, 3), theirs, pl.ds(256 * (i % 2), 256)]

    met_x = set()

    def share_weights(i):
        if i // 2 not in met_x:
            met_x.add(i // 2)
            for d in range(1, 4):
                arrived(wbuf.at[i // 2, d, part], wx_sem.at[1, i // 2, d])
        piece = weights(i, 0)
        for e in (1, 3):
            send(piece, piece, wy_sem.at[0, i, e], wy_sem.at[1, i, e], at(y_=plus(y, e)))

    ahead = 1 + 2 * c

    def pass_weights(i):
        piece = weights(i, ahead)
        arrived(piece, wy_sem.at[1, i, ahead])
        send(piece, piece, wy_sem.at[0, i, 2], wy_sem.at[1, i, 2], at(y_=plus(y, ahead)))

    def await_weights(k):
        local_w[k].wait()
        for i in (2 * k, 2 * k + 1):
            for e in (4 - ahead, 2):
                arrived(weights(i, e), wy_sem.at[1, i, e])

    def pass_context(b):
        arrived(cbuf.at[4 - ahead, b], c_sem.at[1, b, 4 - ahead])
        send(cbuf.at[4 - ahead, b], cbuf.at[2, b], c_sem.at[0, b, 2], c_sem.at[1, b, 2],
             at(x_=plus(x, ahead)))

    def pass_pair(_):
        arrived(kvb.at[1 - mine, rows], kv_sem.at[1])
        send(kvb.at[1 - mine, rows], kvb.at[1 - mine, rows], kv_sem.at[2], kv_sem.at[3], at(1 - c))

    def await_pair(_):
        local_kv.wait()
        local_q.wait()
        other_rows = pl.ds(pl.multiple_of((1 - c) * HALF, HALF), HALF)
        arrived(kvb.at[1 - mine, other_rows], kv_sem.at[3])

    def send_key_weights(_):
        local_kw.wait()
        gain = jnp.broadcast_to(gain_ref[...], (8, COLS)).T[:, :1]
        gkb[z] = (kwb[...].astype(F32) * gain).astype(BF16).reshape(2, 256, KEYS)
        for e in range(1, 4):
            send(gkb.at[z, c, part], gkb.at[z, c, part], gs_sem.at[0, e], gr_sem.at[0, e],
                 at(z_=plus(z, e)))

    def key_weights(e_y):
        theirs = pl.ds(pl.multiple_of(plus(y, 4 - e_y) * 64, 64), 64)
        return [gkb.at[plus(z, e), c, theirs] for e in range(1, 4)]

    def share_key_weights(_):
        for e in range(1, 4):
            arrived(gkb.at[plus(z, 4 - e), c, part], gr_sem.at[0, e])
        for e_y in (1, 3):
            for i, piece in enumerate(key_weights(0)):
                send(piece, piece, gs_sem.at[e_y, i], gr_sem.at[e_y, i], at(y_=plus(y, e_y)))

    def pass_key_weights(_):
        for i, piece in enumerate(key_weights(ahead)):
            arrived(piece, gr_sem.at[ahead, i])
            send(piece, piece, gs_sem.at[2, i], gr_sem.at[2, i], at(y_=plus(y, ahead)))

    def swap_key_weights(_):
        for e_y in (4 - ahead, 2):
            for i, piece in enumerate(key_weights(e_y)):
                arrived(piece, gr_sem.at[e_y, i])
        for e in range(1, 4):
            piece = gkb.at[plus(z, e), c]
            send(piece, piece, gs_sem.at[4, e], gr_sem.at[4, e], at(1 - c))

    def await_key_weights():
        for e in range(1, 4):
            arrived(gkb.at[plus(z, e), 1 - c], gr_sem.at[4, e])

    def attend(index):
        seen = 128 * (index + 1)
        here = pl.ds(128 * index, 128)
        picked = jnp.concatenate([qbuf[here, :HEAD], qbuf[here, HEAD:]], axis=0)
        scores = dot(kvb[0, :seen, :], picked, ((1,), (1,)))
        first = seg_ref[:, here]
        first = jnp.concatenate([first, first], axis=1)
        key_at = lax.broadcasted_iota(jnp.int32, (seen, 256), 0)
        query_at = 128 * index + lax.broadcasted_iota(jnp.int32, (seen, 256), 1) % 128
        scores = jnp.where((key_at >= first) & (key_at <= query_at), scores, MASKED)
        top = jnp.max(scores, axis=0, keepdims=True)
        weights = jnp.exp2((scores - top) * SCALE)
        total = jnp.sum(weights, axis=0, keepdims=True)
        context = dot(kvb[1, :seen, :], weights.astype(BF16), ((0,), (0,)))
        return (context / total).T.astype(BF16)

    def context_block(b):
        for half in range(2):
            context = attend(b + 4 * half)
            there = pl.ds(128 * half, 128)
            cbuf[0, b, there, :HEAD] = context[:128]
            cbuf[0, b, there, HEAD:] = context[128:]
        for d in (1, 3):
            send(cbuf.at[0, b], cbuf.at[d, b], c_sem.at[0, b, d], c_sem.at[1, b, d],
                 at(x_=plus(x, 4 - d)))

    met_k, met_b = set(), set()

    def multiply(u):
        k, b = UNITS[u]
        if k not in met_k:
            met_k.add(k)
            await_weights(k)
        if b not in met_b:
            met_b.add(b)
            arrived(cbuf.at[ahead, b], c_sem.at[1, b, ahead])
            arrived(cbuf.at[2, b], c_sem.at[1, b, 2])
        total = dot(cbuf[0, b], wbuf[k, 0])
        for d in range(1, 4):
            total += dot(cbuf[d, b], wbuf[k, d])
        pbuf[u, 0] = total[:128]
        pbuf[u, 1] = total[128:]
        xsend[u] = pbuf[u, 1 - c].astype(BF16)
        send(xsend.at[u], xrecv.at[u], p_sem.at[0, u], p_sem.at[1, u], at(1 - c))

    def add_half(u):
        k, b = UNITS[u]
        arrived(xrecv.at[u], p_sem.at[1, u])
        total = pbuf[u, c] + xrecv[u].astype(F32)
        if k == 3:
            total += resb[pl.ds(128 * b, 128), :].astype(F32)
        pbuf[u, c] = total

    def pass_on(u):
        k, b = UNITS[u]
        to = owner[k]
        up = to > z
        has = (up & (z > 0)) | (jnp.logical_not(up) & (z < 3))

        @pl.when(has)
        def _():
            arrived(zrecv.at[to, b], zr_sem.at[to, b])
            zsend[k, b] = (pbuf[u, c] + zrecv[to, b].astype(F32)).astype(BF16)

        @pl.when(jnp.logical_not(has))
        def _():
            zsend[k, b] = pbuf[u, c].astype(BF16)

        following = jnp.where(up, z + 1, z - 1)
        slot = jnp.where(jnp.logical_not(up) & (to == following), 4, to)
        send(zsend.at[k, b], zrecv.at[slot, b], zs_sem.at[k, b], zr_sem.at[slot, b],
             at(z_=following))

    locals_ = []

    def hand(b):
        u = UNITS.index((3, b))
        held = pbuf.at[u, 1 - c]
        held[...] = pbuf[u, c]

        @pl.when(z > 0)
        def _():
            arrived(zrecv.at[z, b], zr_sem.at[z, b])
            held[...] += zrecv[z, b].astype(F32)

        @pl.when(z < 3)
        def _():
            arrived(zrecv.at[4, b], zr_sem.at[4, b])
            held[...] += zrecv[4, b].astype(F32)

        hbuf[b] = held[...].astype(BF16)
        place = pl.ds(pl.multiple_of(c * HALF + 128 * b, 128), 128)
        copy = pltpu.make_async_copy(hbuf.at[b], hand_hbm.at[place], hl_sem.at[b])
        copy.start()
        locals_.append(copy)
        send(hbuf.at[b], hand_hbm.at[place], h_sem.at[0, b], h_sem.at[1, b], at(1 - c))
        hidden = hbuf[b].astype(F32)
        sq1[b // 2, x, b % 2] = lax.dot_general(
            jnp.ones((8, COLS), F32), hidden * hidden, (((1,), (1,)), ((), ())),
            precision=lax.Precision.HIGHEST, preferred_element_type=F32,
        )

    met_key_weights = []

    def keys_1(g):
        if not met_key_weights:
            met_key_weights.append(g)
            await_key_weights()
        partial = jnp.zeros((GROUP, KEYS), F32)
        for k in range(4):
            u = UNITS.index((k, 2 * g))
            assert UNITS[u + 1] == (k, 2 * g + 1)
            held = jnp.concatenate([pbuf[u, c], pbuf[u + 1, c]], axis=0).astype(BF16)
            partial += dot(held, gkb[owner[k]].reshape(COLS, KEYS))
        k1s[g] = partial.astype(BF16)
        for d in range(1, 4):
            to = plus(x, 4 - d)
            send(k1s.at[g, pl.ds(pl.multiple_of(to * 64, 64), 64)], k1r.at[g, d],
                 ks_sem.at[0, g, d], kr_sem.at[0, g, d], at(x_=to))

    def keys_2(g):
        total = k1s[g, pl.ds(pl.multiple_of(x * 64, 64), 64), :].astype(F32)
        for d in range(1, 4):
            arrived(k1r.at[g, d], kr_sem.at[0, g, d])
            total += k1r[g, d].astype(F32)
        k2s[g] = total.astype(BF16)
        for e in range(1, 4):
            to = plus(z, e)
            send(k2s.at[g, pl.ds(pl.multiple_of(to * 16, 16), 16)], k2r.at[g, e],
                 ks_sem.at[1, g, e], kr_sem.at[1, g, e], at(z_=to))

    def keys_3(g):
        mine_ = pl.ds(pl.multiple_of(z * 16, 16), 16)
        total = k2s[g, mine_, :].astype(F32)
        for e in range(1, 4):
            arrived(k2r.at[g, e], kr_sem.at[1, g, e])
            total += k2r[g, e].astype(F32)
        place = pl.ds(pl.multiple_of(x * 64 + z * 16, 16), 16)
        k3[g, place, :] = total.astype(BF16)
        for e in range(1, 4):
            send(k3.at[g, place], k3.at[g, place], ks_sem.at[2, g, e], kr_sem.at[2, g, e],
                 at(z_=plus(z, e)))

    def keys_4(g):
        for e in range(1, 4):
            place = pl.ds(pl.multiple_of(x * 64 + plus(z, 4 - e) * 16, 16), 16)
            arrived(k3.at[g, place], kr_sem.at[2, g, e])
        held = k3.at[g, pl.ds(pl.multiple_of(x * 64, 64), 64)]
        place = keys_hbm.at[pl.ds(pl.multiple_of(GROUP * g + x * 64, 64), 64)]
        copy = pltpu.make_async_copy(held, place, kl_sem.at[g])
        copy.start()
        locals_.append(copy)
        for d in range(1, 4):
            send(held, place, ks_sem.at[3, g, d], kr_sem.at[3, g, d], at(x_=plus(x, d)))

    def squares_1(g):
        for d in range(1, 4):
            send(sq1.at[g, x], sq1.at[g, x], qs_sem.at[0, g, d], qr_sem.at[0, g, d],
                 at(x_=plus(x, d)))

    def squares_2(g):
        for d in range(1, 4):
            arrived(sq1.at[g, plus(x, 4 - d)], qr_sem.at[0, g, d])
        sq2[g, z] = (sq1[g, 0] + sq1[g, 1]) + (sq1[g, 2] + sq1[g, 3])
        for e in range(1, 4):
            send(sq2.at[g, z], sq2.at[g, z], qs_sem.at[1, g, e], qr_sem.at[1, g, e],
                 at(z_=plus(z, e)))

    def keys_5(g):
        for d in range(1, 4):
            place = pl.ds(pl.multiple_of(GROUP * g + plus(x, 4 - d) * 64, 64), 64)
            arrived(keys_hbm.at[place], kr_sem.at[3, g, d])
        for e in range(1, 4):
            arrived(sq2.at[g, plus(z, 4 - e)], qr_sem.at[1, g, e])
        squares_ref[g] = (sq2[g, 0] + sq2[g, 1]) + (sq2[g, 2] + sq2[g, 3])

    local_res.wait()
    send_weights(0)
    send_weights(1)
    send_weights(2)
    send_key_weights(0)
    share_weights(0)
    share_weights(1)
    pass_pair(0)
    await_pair(0)
    context_block(3)
    pass_weights(0)
    share_weights(2)
    share_weights(3)
    context_block(1)
    pass_context(3)
    pass_weights(1)
    share_weights(5)
    context_block(2)
    pass_context(1)
    share_weights(4)
    pass_weights(3)
    multiply(3)
    pass_weights(2)
    share_key_weights(0)
    add_half(3)
    pass_weights(5)
    pass_context(2)
    pass_on(3)
    send_weights(3)
    multiply(1)
    context_block(0)
    multiply(2)
    add_half(1)
    pass_on(1)
    multiply(7)
    multiply(5)
    pass_weights(4)
    multiply(6)
    share_weights(6)
    share_weights(7)
    add_half(2)
    pass_on(2)
    pass_key_weights(0)
    add_half(7)
    add_half(5)
    pass_context(0)
    pass_on(7)
    add_half(6)
    multiply(11)
    multiply(10)
    multiply(9)
    pass_on(5)
    pass_weights(6)
    add_half(11)
    multiply(8)
    multiply(0)
    add_half(9)
    multiply(4)
    pass_weights(7)
    add_half(10)
    add_half(8)
    add_half(0)
    pass_on(0)
    swap_key_weights(0)
    pass_on(6)
    pass_on(11)
    multiply(14)
    multiply(15)
    multiply(13)
    pass_on(10)
    multiply(12)
    add_half(14)
    add_half(15)
    keys_1(1)
    add_half(4)
    pass_on(9)
    add_half(13)
    add_half(12)
    keys_1(0)
    hand(3)
    keys_2(1)
    pass_on(4)
    hand(2)
    keys_2(0)
    squares_1(1)
    keys_3(1)
    pass_on(8)
    hand(1)
    keys_3(0)
    squares_2(1)
    keys_4(1)
    hand(0)
    squares_1(0)
    keys_4(0)
    keys_5(1)
    squares_2(0)
    keys_5(0)
    for b in range(4):
        place = pl.ds(pl.multiple_of((1 - c) * HALF + 128 * b, 128), 128)
        arrived(hand_hbm.at[place], h_sem.at[1, b])
    for copy in locals_:
        copy.wait()
    for copy in started:
        copy.wait_send()


def rotation():
    angles = np.arange(LEN)[:, None] * THETA ** (-2.0 * np.arange(HEAD // 2) / HEAD)[None, :]
    cosine, sine = np.cos(angles), np.sin(angles)
    return np.stack(
        [np.concatenate([cosine, cosine], 1), np.concatenate([-sine, sine], 1)]
    ).astype(np.float32)


def deliver(hand_in, keys_in, squares_ref, bias_ref, rot_hbm, hand_out, keys_out, hand, keys, out, rot, sem):
    rows = [pl.ds(256 * i, 256) for i in range(4)]
    half = pl.ds(pl.multiple_of(lax.axis_index("section") * HALF, HALF), HALF)
    first = [pltpu.make_async_copy(hand_in.at[r], hand.at[r], sem.at[0, i]) for i, r in enumerate(rows)]
    second = [pltpu.make_async_copy(hand.at[r], hand_out.at[r], sem.at[1, i]) for i, r in enumerate(rows)]
    keys_first = [pltpu.make_async_copy(keys_in.at[r], keys.at[r], sem.at[0, 4 + i]) for i, r in enumerate(rows[:2])]
    keys_second = [pltpu.make_async_copy(out.at[r], keys_out.at[r], sem.at[1, 4 + i]) for i, r in enumerate(rows[:2])]
    angles = pltpu.make_async_copy(rot_hbm.at[:, half], rot, sem.at[0, 6])
    for copy in [*first, *keys_first, angles]:
        copy.start()
    for arriving, leaving in zip(first, second, strict=True):
        arriving.wait()
        leaving.start()
    inverse = lax.rsqrt(squares_ref[...] / D + EPS)
    angles.wait()
    for g in range(2):
        keys_first[g].wait()
        for i in range(2):
            at_rows = pl.ds(GROUP * g + 128 * i, 128)
            projected = keys[at_rows, :].astype(F32) * inverse[g, i].T[:, :1] + bias_ref[...]
            cosine, sine = rot[0, at_rows, :], rot[1, at_rows, :]
            for head in range(KEYS // HEAD):
                v = projected[:, head * HEAD : (head + 1) * HEAD]
                crossed = jnp.concatenate([v[:, HEAD // 2 :], v[:, : HEAD // 2]], axis=1)
                out[at_rows, pl.ds(head * HEAD, HEAD)] = (v * cosine + crossed * sine).astype(BF16)
        keys_second[g].start()
    for copy in second + keys_second:
        copy.wait()


def local(queries, keys_values, segments, residual, out_weight, key_weight, key_bias, norm_gain):
    hbm = pl.BlockSpec(memory_space=pl.ANY)
    vmem = pl.BlockSpec(memory_space=pltpu.VMEM)
    dma = pltpu.SemaphoreType.DMA
    handed, keys, squares = pl.pallas_call(
        kernel,
        out_shape=(
            jax.ShapeDtypeStruct((LEN, COLS), BF16),
            jax.ShapeDtypeStruct((HALF, KEYS), BF16),
            jax.ShapeDtypeStruct((2, 2, 8, 128), F32),
        ),
        in_specs=[hbm, hbm, vmem, hbm, hbm, hbm, vmem],
        out_specs=(hbm, hbm, vmem),
        scratch_shapes=[
            pltpu.VMEM((LEN, 256), BF16),
            pltpu.VMEM((2, LEN, HEAD), BF16),
            pltpu.VMEM((4, 4, 256, COLS), BF16),
            pltpu.VMEM((HALF, COLS), BF16),
            pltpu.VMEM((COLS, KEYS), BF16),
            pltpu.VMEM((4, 2, 256, KEYS), BF16),
            pltpu.VMEM((4, 4, 256, 256), BF16),
            pltpu.VMEM((16, 2, 128, COLS), F32),
            pltpu.VMEM((16, 128, COLS), BF16),
            pltpu.VMEM((16, 128, COLS), BF16),
            pltpu.VMEM((3, 4, 128, COLS), BF16),
            pltpu.VMEM((5, 4, 128, COLS), BF16),
            pltpu.VMEM((4, 128, COLS), BF16),
            pltpu.VMEM((2, GROUP, KEYS), BF16),
            pltpu.VMEM((2, 4, 64, KEYS), BF16),
            pltpu.VMEM((2, 64, KEYS), BF16),
            pltpu.VMEM((2, 4, 16, KEYS), BF16),
            pltpu.VMEM((2, GROUP, KEYS), BF16),
            pltpu.VMEM((2, 4, 2, 8, 128), F32),
            pltpu.VMEM((2, 4, 2, 8, 128), F32),
            dma((6,)),
            dma((4,)),
            dma((4,)),
            dma((2, 4, 4)),
            dma((2, 8, 4)),
            dma((2, 4, 4)),
            dma((2, 16)),
            dma((3, 4)),
            dma((5, 4)),
            dma((2, 4)),
            dma((4,)),
            dma((5, 4)),
            dma((5, 4)),
            dma((4, 2, 4)),
            dma((4, 2, 4)),
            dma((2,)),
            dma((2, 2, 4)),
            dma((2, 2, 4)),
        ],
        compiler_params=pltpu.CompilerParams(
            collective_id=0, has_side_effects=True, vmem_limit_bytes=56 << 20
        ),
        name="relay",
    )(
        queries[0], keys_values[0], segments, residual[0], out_weight, key_weight,
        norm_gain.reshape(1, COLS),
    )
    handed, keys = pl.pallas_call(
        deliver,
        out_shape=(
            jax.ShapeDtypeStruct((LEN, COLS), BF16),
            jax.ShapeDtypeStruct((HALF, KEYS), BF16),
        ),
        in_specs=[hbm, hbm, vmem, vmem, hbm],
        out_specs=(hbm, hbm),
        scratch_shapes=[
            pltpu.VMEM((LEN, COLS), BF16),
            pltpu.VMEM((HALF, KEYS), BF16),
            pltpu.VMEM((HALF, KEYS), BF16),
            pltpu.VMEM((2, HALF, HEAD), F32),
            dma((2, 7)),
        ],
        compiler_params=pltpu.CompilerParams(vmem_limit_bytes=60 << 20),
        name="deliver",
    )(handed, keys, squares, key_bias.reshape(1, KEYS), jnp.asarray(rotation()))
    return handed[None], keys[None]


def solution(mesh):
    return jax.shard_map(
        local,
        mesh=mesh,
        in_specs=(
            P("narrow", None, "wide"),
            P("narrow", None, "wide"),
            P("narrow", None),
            P("narrow", None, "wide"),
            P("wide", None),
            P("wide", None),
            P(),
            P("wide"),
        ),
        out_specs=(P("narrow", None, "wide"), P("narrow", "section", None)),
        check_vma=False,
    )
```

```python
import functools
import math

import jax
import jax.numpy as jnp
import numpy as np
from jax import lax
from jax.experimental import pallas as pl
from jax.experimental.pallas import tpu as pltpu
from jax.sharding import PartitionSpec as P

MESH = pl.DeviceIdType.MESH
D = 8192
HEAD = 128
LEN = 1024
HALF = LEN // 2
COLS = 512
KEYS = 512
THETA = 1000000.0
EPS = 1e-06
MASKED = -1e30
SCALE = math.log2(math.e) / math.sqrt(HEAD)
BF16 = jnp.bfloat16
F32 = jnp.float32
GROUP = 256
UNITS = [(k, b) for k in range(4) for b in range(4)]


def dot(a, b, dims=((1,), (0,))):
    return lax.dot_general(a, b, (dims, ((), ())), preferred_element_type=F32)


def kernel(
    q_hbm, kv_hbm, seg_ref, res_hbm, w_hbm, kw_hbm, gain_ref,
    hand_hbm, keys_hbm, squares_ref,
    qbuf, kvb, wbuf, resb, kwb, gkb, cbuf, pbuf, xsend, xrecv, zsend, zrecv, hbuf,
    k1s, k1r, k2s, k2r, k3, sq1, sq2,
    l_sem, wl_sem, kv_sem, wx_sem, wy_sem, c_sem, p_sem, zs_sem, zr_sem, h_sem, hl_sem,
    gs_sem, gr_sem, ks_sem, kr_sem, kl_sem, qs_sem, qr_sem,
):
    c = lax.axis_index("section")
    w = lax.axis_index("wide")
    n = lax.axis_index("narrow")
    x, z = w // 4, w % 4
    y, h = n // 2, n % 2

    def at(c_=None, x_=None, y_=None, z_=None):
        xx = x if x_ is None else x_
        zz = z if z_ is None else z_
        yy = y if y_ is None else y_
        return {"section": c if c_ is None else c_, "wide": xx * 4 + zz, "narrow": yy * 2 + h}

    def plus(value, by):
        return (value + by) % 4

    started = []

    def send(src, dst, send_sem, recv_sem, to):
        copy = pltpu.make_async_remote_copy(
            src_ref=src, dst_ref=dst, send_sem=send_sem, recv_sem=recv_sem,
            device_id=to, device_id_type=MESH,
        )
        copy.start()
        started.append(copy)

    def arrived(dst, recv_sem):
        pltpu.make_async_remote_copy(
            src_ref=dst, dst_ref=dst, send_sem=recv_sem, recv_sem=recv_sem,
            device_id=at(1 - c), device_id_type=MESH,
        ).wait_recv()

    barrier = pltpu.get_barrier_semaphore()
    partners = [at(1 - c)]
    for d in range(1, 4):
        partners += [at(x_=plus(x, d)), at(y_=plus(y, d)), at(z_=plus(z, d))]
    for to in partners:
        pl.semaphore_signal(barrier, inc=1, device_id=to, device_id_type=MESH)

    owner = [3 * (1 - z // 2), (2 + 3 * z) % 5, 1 + z % 2, z]
    pair = z + 1 - 2 * (z % 2)
    mine = z % 2
    rows = pl.ds(pl.multiple_of(c * HALF, HALF), HALF)

    heads = pl.ds(pl.multiple_of(c * 256, 256), 256)
    local_kv = pltpu.make_async_copy(kv_hbm, kvb.at[mine], l_sem.at[0])
    local_q = pltpu.make_async_copy(q_hbm.at[:, heads], qbuf, l_sem.at[1])
    local_res = pltpu.make_async_copy(res_hbm.at[rows], resb, l_sem.at[2])
    local_kw = pltpu.make_async_copy(kw_hbm, kwb, l_sem.at[3])
    def columns(k, x_):
        return pl.ds(pl.multiple_of(x_ * (4 * COLS) + owner[k] * COLS, COLS), COLS)

    local_w = [
        pltpu.make_async_copy(w_hbm.at[heads, columns(k, x)], wbuf.at[k, 0], wl_sem.at[k])
        for k in range(4)
    ]
    for copy in [local_kv, local_kw, local_q, *local_w, local_res]:
        copy.start()

    pl.semaphore_wait(barrier, len(partners))

    send(kv_hbm.at[rows], kvb.at[mine, rows], kv_sem.at[0], kv_sem.at[1], at(z_=pair))
    part = pl.ds(pl.multiple_of(y * 64, 64), 64)
    w_rows = pl.ds(pl.multiple_of(c * 256 + y * 64, 64), 64)

    def send_weights(k):
        for d in range(1, 4):
            to = plus(x, 4 - d)
            send(w_hbm.at[w_rows, columns(k, to)], wbuf.at[k, d, part],
                 wx_sem.at[0, k, d], wx_sem.at[1, k, d], at(x_=to))

    def weights(i, e):
        theirs = pl.ds(pl.multiple_of(plus(y, 4 - e) * 64, 64), 64)
        return wbuf.at[i // 2, pl.ds(1, 3), theirs, pl.ds(256 * (i % 2), 256)]

    met_x = set()

    def share_weights(i):
        if i // 2 not in met_x:
            met_x.add(i // 2)
            for d in range(1, 4):
                arrived(wbuf.at[i // 2, d, part], wx_sem.at[1, i // 2, d])
        piece = weights(i, 0)
        for e in (1, 3):
            send(piece, piece, wy_sem.at[0, i, e], wy_sem.at[1, i, e], at(y_=plus(y, e)))

    ahead = 1 + 2 * c

    def pass_weights(i):
        piece = weights(i, ahead)
        arrived(piece, wy_sem.at[1, i, ahead])
        send(piece, piece, wy_sem.at[0, i, 2], wy_sem.at[1, i, 2], at(y_=plus(y, ahead)))

    def await_weights(k):
        local_w[k].wait()
        for i in (2 * k, 2 * k + 1):
            for e in (4 - ahead, 2):
                arrived(weights(i, e), wy_sem.at[1, i, e])

    def pass_context(b):
        arrived(cbuf.at[4 - ahead, b], c_sem.at[1, b, 4 - ahead])
        send(cbuf.at[4 - ahead, b], cbuf.at[2, b], c_sem.at[0, b, 2], c_sem.at[1, b, 2],
             at(x_=plus(x, ahead)))

    def pass_pair(_):
        arrived(kvb.at[1 - mine, rows], kv_sem.at[1])
        send(kvb.at[1 - mine, rows], kvb.at[1 - mine, rows], kv_sem.at[2], kv_sem.at[3], at(1 - c))

    def await_pair(_):
        local_kv.wait()
        local_q.wait()
        other_rows = pl.ds(pl.multiple_of((1 - c) * HALF, HALF), HALF)
        arrived(kvb.at[1 - mine, other_rows], kv_sem.at[3])

    def send_key_weights(_):
        local_kw.wait()
        gain = jnp.broadcast_to(gain_ref[...], (8, COLS)).T[:, :1]
        gkb[z] = (kwb[...].astype(F32) * gain).astype(BF16).reshape(2, 256, KEYS)
        for e in range(1, 4):
            send(gkb.at[z, c, part], gkb.at[z, c, part], gs_sem.at[0, e], gr_sem.at[0, e],
                 at(z_=plus(z, e)))

    def key_weights(e_y):
        theirs = pl.ds(pl.multiple_of(plus(y, 4 - e_y) * 64, 64), 64)
        return [gkb.at[plus(z, e), c, theirs] for e in range(1, 4)]

    def share_key_weights(_):
        for e in range(1, 4):
            arrived(gkb.at[plus(z, 4 - e), c, part], gr_sem.at[0, e])
        for e_y in (1, 3):
            for i, piece in enumerate(key_weights(0)):
                send(piece, piece, gs_sem.at[e_y, i], gr_sem.at[e_y, i], at(y_=plus(y, e_y)))

    def pass_key_weights(_):
        for i, piece in enumerate(key_weights(ahead)):
            arrived(piece, gr_sem.at[ahead, i])
            send(piece, piece, gs_sem.at[2, i], gr_sem.at[2, i], at(y_=plus(y, ahead)))

    def swap_key_weights(_):
        for e_y in (4 - ahead, 2):
            for i, piece in enumerate(key_weights(e_y)):
                arrived(piece, gr_sem.at[e_y, i])
        for e in range(1, 4):
            piece = gkb.at[plus(z, e), c]
            send(piece, piece, gs_sem.at[4, e], gr_sem.at[4, e], at(1 - c))

    def await_key_weights():
        for e in range(1, 4):
            arrived(gkb.at[plus(z, e), 1 - c], gr_sem.at[4, e])

    def attend(index):
        seen = 128 * (index + 1)
        here = pl.ds(128 * index, 128)
        picked = jnp.concatenate([qbuf[here, :HEAD], qbuf[here, HEAD:]], axis=0)
        scores = dot(kvb[0, :seen, :], picked, ((1,), (1,)))
        first = seg_ref[:, here]
        first = jnp.concatenate([first, first], axis=1)
        key_at = lax.broadcasted_iota(jnp.int32, (seen, 256), 0)
        query_at = 128 * index + lax.broadcasted_iota(jnp.int32, (seen, 256), 1) % 128
        scores = jnp.where((key_at >= first) & (key_at <= query_at), scores, MASKED)
        top = jnp.max(scores, axis=0, keepdims=True)
        weights = jnp.exp2((scores - top) * SCALE)
        total = jnp.sum(weights, axis=0, keepdims=True)
        context = dot(kvb[1, :seen, :], weights.astype(BF16), ((0,), (0,)))
        return (context / total).T.astype(BF16)

    def context_block(b):
        for half in range(2):
            context = attend(b + 4 * half)
            there = pl.ds(128 * half, 128)
            cbuf[0, b, there, :HEAD] = context[:128]
            cbuf[0, b, there, HEAD:] = context[128:]
        for d in (1, 3):
            send(cbuf.at[0, b], cbuf.at[d, b], c_sem.at[0, b, d], c_sem.at[1, b, d],
                 at(x_=plus(x, 4 - d)))

    met_k, met_b = set(), set()

    def multiply(u):
        k, b = UNITS[u]
        if k not in met_k:
            met_k.add(k)
            await_weights(k)
        if b not in met_b:
            met_b.add(b)
            arrived(cbuf.at[ahead, b], c_sem.at[1, b, ahead])
            arrived(cbuf.at[2, b], c_sem.at[1, b, 2])
        total = dot(cbuf[0, b], wbuf[k, 0])
        for d in range(1, 4):
            total += dot(cbuf[d, b], wbuf[k, d])
        pbuf[u, 0] = total[:128]
        pbuf[u, 1] = total[128:]
        xsend[u] = pbuf[u, 1 - c].astype(BF16)
        send(xsend.at[u], xrecv.at[u], p_sem.at[0, u], p_sem.at[1, u], at(1 - c))

    def add_half(u):
        k, b = UNITS[u]
        arrived(xrecv.at[u], p_sem.at[1, u])
        total = pbuf[u, c] + xrecv[u].astype(F32)
        if k == 3:
            total += resb[pl.ds(128 * b, 128), :].astype(F32)
        pbuf[u, c] = total

    def pass_on(u):
        k, b = UNITS[u]
        to = owner[k]
        up = to > z
        has = (up & (z > 0)) | (jnp.logical_not(up) & (z < 3))

        @pl.when(has)
        def _():
            arrived(zrecv.at[to, b], zr_sem.at[to, b])
            zsend[k, b] = (pbuf[u, c] + zrecv[to, b].astype(F32)).astype(BF16)

        @pl.when(jnp.logical_not(has))
        def _():
            zsend[k, b] = pbuf[u, c].astype(BF16)

        following = jnp.where(up, z + 1, z - 1)
        slot = jnp.where(jnp.logical_not(up) & (to == following), 4, to)
        send(zsend.at[k, b], zrecv.at[slot, b], zs_sem.at[k, b], zr_sem.at[slot, b],
             at(z_=following))

    locals_ = []

    def hand(b):
        u = UNITS.index((3, b))
        held = pbuf.at[u, 1 - c]
        held[...] = pbuf[u, c]

        @pl.when(z > 0)
        def _():
            arrived(zrecv.at[z, b], zr_sem.at[z, b])
            held[...] += zrecv[z, b].astype(F32)

        @pl.when(z < 3)
        def _():
            arrived(zrecv.at[4, b], zr_sem.at[4, b])
            held[...] += zrecv[4, b].astype(F32)

        hbuf[b] = held[...].astype(BF16)
        place = pl.ds(pl.multiple_of(c * HALF + 128 * b, 128), 128)
        copy = pltpu.make_async_copy(hbuf.at[b], hand_hbm.at[place], hl_sem.at[b])
        copy.start()
        locals_.append(copy)
        send(hbuf.at[b], hand_hbm.at[place], h_sem.at[0, b], h_sem.at[1, b], at(1 - c))
        hidden = hbuf[b].astype(F32)
        sq1[b // 2, x, b % 2] = lax.dot_general(
            jnp.ones((8, COLS), F32), hidden * hidden, (((1,), (1,)), ((), ())),
            precision=lax.Precision.HIGHEST, preferred_element_type=F32,
        )

    met_key_weights = []

    def keys_1(g):
        if not met_key_weights:
            met_key_weights.append(g)
            await_key_weights()
        partial = jnp.zeros((GROUP, KEYS), F32)
        for k in range(4):
            u = UNITS.index((k, 2 * g))
            assert UNITS[u + 1] == (k, 2 * g + 1)
            held = jnp.concatenate([pbuf[u, c], pbuf[u + 1, c]], axis=0).astype(BF16)
            partial += dot(held, gkb[owner[k]].reshape(COLS, KEYS))
        k1s[g] = partial.astype(BF16)
        for d in range(1, 4):
            to = plus(x, 4 - d)
            send(k1s.at[g, pl.ds(pl.multiple_of(to * 64, 64), 64)], k1r.at[g, d],
                 ks_sem.at[0, g, d], kr_sem.at[0, g, d], at(x_=to))

    def keys_2(g):
        total = k1s[g, pl.ds(pl.multiple_of(x * 64, 64), 64), :].astype(F32)
        for d in range(1, 4):
            arrived(k1r.at[g, d], kr_sem.at[0, g, d])
            total += k1r[g, d].astype(F32)
        k2s[g] = total.astype(BF16)
        for e in range(1, 4):
            to = plus(z, e)
            send(k2s.at[g, pl.ds(pl.multiple_of(to * 16, 16), 16)], k2r.at[g, e],
                 ks_sem.at[1, g, e], kr_sem.at[1, g, e], at(z_=to))

    def keys_3(g):
        mine_ = pl.ds(pl.multiple_of(z * 16, 16), 16)
        total = k2s[g, mine_, :].astype(F32)
        for e in range(1, 4):
            arrived(k2r.at[g, e], kr_sem.at[1, g, e])
            total += k2r[g, e].astype(F32)
        place = pl.ds(pl.multiple_of(x * 64 + z * 16, 16), 16)
        k3[g, place, :] = total.astype(BF16)
        for e in range(1, 4):
            send(k3.at[g, place], k3.at[g, place], ks_sem.at[2, g, e], kr_sem.at[2, g, e],
                 at(z_=plus(z, e)))

    def keys_4(g):
        for e in range(1, 4):
            place = pl.ds(pl.multiple_of(x * 64 + plus(z, 4 - e) * 16, 16), 16)
            arrived(k3.at[g, place], kr_sem.at[2, g, e])
        held = k3.at[g, pl.ds(pl.multiple_of(x * 64, 64), 64)]
        place = keys_hbm.at[pl.ds(pl.multiple_of(GROUP * g + x * 64, 64), 64)]
        copy = pltpu.make_async_copy(held, place, kl_sem.at[g])
        copy.start()
        locals_.append(copy)
        for d in range(1, 4):
            send(held, place, ks_sem.at[3, g, d], kr_sem.at[3, g, d], at(x_=plus(x, d)))

    def squares_1(g):
        for d in range(1, 4):
            send(sq1.at[g, x], sq1.at[g, x], qs_sem.at[0, g, d], qr_sem.at[0, g, d],
                 at(x_=plus(x, d)))

    def squares_2(g):
        for d in range(1, 4):
            arrived(sq1.at[g, plus(x, 4 - d)], qr_sem.at[0, g, d])
        sq2[g, z] = (sq1[g, 0] + sq1[g, 1]) + (sq1[g, 2] + sq1[g, 3])
        for e in range(1, 4):
            send(sq2.at[g, z], sq2.at[g, z], qs_sem.at[1, g, e], qr_sem.at[1, g, e],
                 at(z_=plus(z, e)))

    def keys_5(g):
        for d in range(1, 4):
            place = pl.ds(pl.multiple_of(GROUP * g + plus(x, 4 - d) * 64, 64), 64)
            arrived(keys_hbm.at[place], kr_sem.at[3, g, d])
        for e in range(1, 4):
            arrived(sq2.at[g, plus(z, 4 - e)], qr_sem.at[1, g, e])
        squares_ref[g] = (sq2[g, 0] + sq2[g, 1]) + (sq2[g, 2] + sq2[g, 3])

    local_res.wait()
    send_weights(0)
    send_weights(1)
    send_weights(2)
    send_key_weights(0)
    share_weights(0)
    share_weights(1)
    pass_pair(0)
    await_pair(0)
    context_block(3)
    pass_weights(0)
    share_weights(2)
    share_weights(3)
    context_block(1)
    pass_context(3)
    pass_weights(1)
    share_weights(5)
    context_block(2)
    pass_context(1)
    share_weights(4)
    pass_weights(3)
    multiply(3)
    pass_weights(2)
    share_key_weights(0)
    add_half(3)
    pass_weights(5)
    pass_context(2)
    pass_on(3)
    send_weights(3)
    multiply(1)
    context_block(0)
    multiply(2)
    add_half(1)
    pass_on(1)
    multiply(7)
    multiply(5)
    pass_weights(4)
    multiply(6)
    share_weights(6)
    share_weights(7)
    add_half(2)
    pass_on(2)
    pass_key_weights(0)
    add_half(7)
    add_half(5)
    pass_context(0)
    pass_on(7)
    add_half(6)
    multiply(11)
    multiply(10)
    multiply(9)
    pass_on(5)
    pass_weights(6)
    add_half(11)
    multiply(8)
    multiply(0)
    add_half(9)
    multiply(4)
    pass_weights(7)
    add_half(10)
    add_half(8)
    add_half(0)
    pass_on(0)
    swap_key_weights(0)
    pass_on(6)
    pass_on(11)
    multiply(14)
    multiply(15)
    multiply(13)
    pass_on(10)
    multiply(12)
    add_half(14)
    add_half(15)
    keys_1(1)
    add_half(4)
    pass_on(9)
    add_half(13)
    add_half(12)
    keys_1(0)
    hand(3)
    keys_2(1)
    pass_on(4)
    hand(2)
    keys_2(0)
    squares_1(1)
    keys_3(1)
    pass_on(8)
    hand(1)
    keys_3(0)
    squares_2(1)
    keys_4(1)
    hand(0)
    squares_1(0)
    keys_4(0)
    keys_5(1)
    squares_2(0)
    keys_5(0)
    for b in range(4):
        place = pl.ds(pl.multiple_of((1 - c) * HALF + 128 * b, 128), 128)
        arrived(hand_hbm.at[place], h_sem.at[1, b])
    for copy in locals_:
        copy.wait()
    for copy in started:
        copy.wait_send()


def rotation():
    angles = np.arange(LEN)[:, None] * THETA ** (-2.0 * np.arange(HEAD // 2) / HEAD)[None, :]
    cosine, sine = np.cos(angles), np.sin(angles)
    return np.stack(
        [np.concatenate([cosine, cosine], 1), np.concatenate([-sine, sine], 1)]
    ).astype(np.float32)


def deliver(
    hand_in, keys_in, squares_hbm, bias_hbm, rot_hbm, hand_out, keys_out,
    hand, keys, out, rot, squares_ref, bias_ref, sem,
):
    rows = [pl.ds(256 * i, 256) for i in range(4)]
    half = pl.ds(pl.multiple_of(lax.axis_index("section") * HALF, HALF), HALF)
    first = [pltpu.make_async_copy(hand_in.at[r], hand.at[r], sem.at[0, i]) for i, r in enumerate(rows)]
    second = [pltpu.make_async_copy(hand.at[r], hand_out.at[r], sem.at[1, i]) for i, r in enumerate(rows)]
    keys_first = [pltpu.make_async_copy(keys_in.at[r], keys.at[r], sem.at[0, 4 + i]) for i, r in enumerate(rows[:2])]
    keys_second = [pltpu.make_async_copy(out.at[r], keys_out.at[r], sem.at[1, 4 + i]) for i, r in enumerate(rows[:2])]
    angles = pltpu.make_async_copy(rot_hbm.at[:, half], rot, sem.at[0, 6])
    small = [
        pltpu.make_async_copy(squares_hbm, squares_ref, sem.at[0, 7]),
        pltpu.make_async_copy(bias_hbm, bias_ref, sem.at[0, 8]),
    ]
    for copy in [*first, *small, *keys_first, angles]:
        copy.start()
    for arriving, leaving in zip(first, second, strict=True):
        arriving.wait()
        leaving.start()
    for copy in small:
        copy.wait()
    inverse = lax.rsqrt(squares_ref[...] / D + EPS)
    angles.wait()
    for g in range(2):
        keys_first[g].wait()
        for i in range(2):
            at_rows = pl.ds(GROUP * g + 128 * i, 128)
            projected = keys[at_rows, :].astype(F32) * inverse[g, i].T[:, :1] + bias_ref[...]
            cosine, sine = rot[0, at_rows, :], rot[1, at_rows, :]
            for head in range(KEYS // HEAD):
                v = projected[:, head * HEAD : (head + 1) * HEAD]
                crossed = jnp.concatenate([v[:, HEAD // 2 :], v[:, : HEAD // 2]], axis=1)
                out[at_rows, pl.ds(head * HEAD, HEAD)] = (v * cosine + crossed * sine).astype(BF16)
        keys_second[g].start()
    for copy in second + keys_second:
        copy.wait()


def local(queries, keys_values, segments, residual, out_weight, key_weight, key_bias, norm_gain):
    hbm = pl.BlockSpec(memory_space=pl.ANY)
    vmem = pl.BlockSpec(memory_space=pltpu.VMEM)
    dma = pltpu.SemaphoreType.DMA
    handed, keys, squares = pl.pallas_call(
        kernel,
        out_shape=(
            jax.ShapeDtypeStruct((LEN, COLS), BF16),
            jax.ShapeDtypeStruct((HALF, KEYS), BF16),
            jax.ShapeDtypeStruct((2, 2, 8, 128), F32),
        ),
        in_specs=[hbm, hbm, vmem, hbm, hbm, hbm, vmem],
        out_specs=(hbm, hbm, vmem),
        scratch_shapes=[
            pltpu.VMEM((LEN, 256), BF16),
            pltpu.VMEM((2, LEN, HEAD), BF16),
            pltpu.VMEM((4, 4, 256, COLS), BF16),
            pltpu.VMEM((HALF, COLS), BF16),
            pltpu.VMEM((COLS, KEYS), BF16),
            pltpu.VMEM((4, 2, 256, KEYS), BF16),
            pltpu.VMEM((4, 4, 256, 256), BF16),
            pltpu.VMEM((16, 2, 128, COLS), F32),
            pltpu.VMEM((16, 128, COLS), BF16),
            pltpu.VMEM((16, 128, COLS), BF16),
            pltpu.VMEM((3, 4, 128, COLS), BF16),
            pltpu.VMEM((5, 4, 128, COLS), BF16),
            pltpu.VMEM((4, 128, COLS), BF16),
            pltpu.VMEM((2, GROUP, KEYS), BF16),
            pltpu.VMEM((2, 4, 64, KEYS), BF16),
            pltpu.VMEM((2, 64, KEYS), BF16),
            pltpu.VMEM((2, 4, 16, KEYS), BF16),
            pltpu.VMEM((2, GROUP, KEYS), BF16),
            pltpu.VMEM((2, 4, 2, 8, 128), F32),
            pltpu.VMEM((2, 4, 2, 8, 128), F32),
            dma((6,)),
            dma((4,)),
            dma((4,)),
            dma((2, 4, 4)),
            dma((2, 8, 4)),
            dma((2, 4, 4)),
            dma((2, 16)),
            dma((3, 4)),
            dma((5, 4)),
            dma((2, 4)),
            dma((4,)),
            dma((5, 4)),
            dma((5, 4)),
            dma((4, 2, 4)),
            dma((4, 2, 4)),
            dma((2,)),
            dma((2, 2, 4)),
            dma((2, 2, 4)),
        ],
        compiler_params=pltpu.CompilerParams(
            collective_id=0, has_side_effects=True, vmem_limit_bytes=56 << 20
        ),
        name="relay",
    )(
        queries[0], keys_values[0], segments, residual[0], out_weight, key_weight,
        norm_gain.reshape(1, COLS),
    )
    handed, keys = pl.pallas_call(
        deliver,
        out_shape=(
            jax.ShapeDtypeStruct((LEN, COLS), BF16),
            jax.ShapeDtypeStruct((HALF, KEYS), BF16),
        ),
        in_specs=[hbm, hbm, hbm, hbm, hbm],
        out_specs=(hbm, hbm),
        scratch_shapes=[
            pltpu.VMEM((LEN, COLS), BF16),
            pltpu.VMEM((HALF, KEYS), BF16),
            pltpu.VMEM((HALF, KEYS), BF16),
            pltpu.VMEM((2, HALF, HEAD), F32),
            pltpu.VMEM((2, 2, 8, 128), F32),
            pltpu.VMEM((1, KEYS), F32),
            dma((2, 9)),
        ],
        compiler_params=pltpu.CompilerParams(vmem_limit_bytes=60 << 20),
        name="deliver",
    )(handed, keys, squares, key_bias.reshape(1, KEYS), jnp.asarray(rotation()))
    return handed[None], keys[None]


def solution(mesh):
    return jax.shard_map(
        local,
        mesh=mesh,
        in_specs=(
            P("narrow", None, "wide"),
            P("narrow", None, "wide"),
            P("narrow", None),
            P("narrow", None, "wide"),
            P("wide", None),
            P("wide", None),
            P(),
            P("wide"),
        ),
        out_specs=(P("narrow", None, "wide"), P("narrow", "section", None)),
        check_vma=False,
    )
```

```python
import functools
import math

import jax
import jax.numpy as jnp
import numpy as np
from jax import lax
from jax.experimental import pallas as pl
from jax.experimental.pallas import tpu as pltpu
from jax.sharding import PartitionSpec as P

MESH = pl.DeviceIdType.MESH
D = 8192
HEAD = 128
LEN = 1024
HALF = LEN // 2
COLS = 512
KEYS = 512
THETA = 1000000.0
EPS = 1e-06
MASKED = -1e30
SCALE = math.log2(math.e) / math.sqrt(HEAD)
BF16 = jnp.bfloat16
F32 = jnp.float32
GROUP = 256
UNITS = [(k, b) for k in range(4) for b in range(4)]


def dot(a, b, dims=((1,), (0,))):
    return lax.dot_general(a, b, (dims, ((), ())), preferred_element_type=F32)


def kernel(
    q_hbm, kv_hbm, seg_ref, res_hbm, w_hbm, kw_hbm, gain_ref,
    hand_hbm, keys_hbm, squares_ref,
    qbuf, kvb, wbuf, resb, kwb, gkb, cbuf, pbuf, xsend, xrecv, zsend, zrecv, hbuf,
    k1s, k1r, k2s, k2r, k3, sq1, sq2,
    l_sem, wl_sem, kv_sem, wx_sem, wy_sem, c_sem, p_sem, zs_sem, zr_sem, h_sem, hl_sem,
    gs_sem, gr_sem, ks_sem, kr_sem, kl_sem, qs_sem, qr_sem,
):
    c = lax.axis_index("section")
    w = lax.axis_index("wide")
    n = lax.axis_index("narrow")
    x, z = w // 4, w % 4
    y, h = n // 2, n % 2

    def at(c_=None, x_=None, y_=None, z_=None):
        xx = x if x_ is None else x_
        zz = z if z_ is None else z_
        yy = y if y_ is None else y_
        return {"section": c if c_ is None else c_, "wide": xx * 4 + zz, "narrow": yy * 2 + h}

    def plus(value, by):
        return (value + by) % 4

    started = []

    def send(src, dst, send_sem, recv_sem, to):
        copy = pltpu.make_async_remote_copy(
            src_ref=src, dst_ref=dst, send_sem=send_sem, recv_sem=recv_sem,
            device_id=to, device_id_type=MESH,
        )
        copy.start()
        started.append(copy)

    def arrived(dst, recv_sem):
        pltpu.make_async_remote_copy(
            src_ref=dst, dst_ref=dst, send_sem=recv_sem, recv_sem=recv_sem,
            device_id=at(1 - c), device_id_type=MESH,
        ).wait_recv()

    barrier = pltpu.get_barrier_semaphore()
    partners = [at(1 - c)]
    for d in range(1, 4):
        partners += [at(x_=plus(x, d)), at(y_=plus(y, d)), at(z_=plus(z, d))]
    for to in partners:
        pl.semaphore_signal(barrier, inc=1, device_id=to, device_id_type=MESH)

    owner = [3 * (1 - z // 2), (2 + 3 * z) % 5, 1 + z % 2, z]
    pair = z + 1 - 2 * (z % 2)
    mine = z % 2
    rows = pl.ds(pl.multiple_of(c * HALF, HALF), HALF)

    heads = pl.ds(pl.multiple_of(c * 256, 256), 256)
    local_kv = pltpu.make_async_copy(kv_hbm, kvb.at[mine], l_sem.at[0])
    local_q = pltpu.make_async_copy(q_hbm.at[:, heads], qbuf, l_sem.at[1])
    local_res = pltpu.make_async_copy(res_hbm.at[rows], resb, l_sem.at[2])
    local_kw = pltpu.make_async_copy(kw_hbm, kwb, l_sem.at[3])
    def columns(k, x_):
        return pl.ds(pl.multiple_of(x_ * (4 * COLS) + owner[k] * COLS, COLS), COLS)

    local_w = [
        pltpu.make_async_copy(w_hbm.at[heads, columns(k, x)], wbuf.at[k, 0], wl_sem.at[k])
        for k in range(4)
    ]
    for copy in [local_kv, local_kw, local_q, *local_w, local_res]:
        copy.start()

    pl.semaphore_wait(barrier, len(partners))

    send(kv_hbm.at[rows], kvb.at[mine, rows], kv_sem.at[0], kv_sem.at[1], at(z_=pair))
    part = pl.ds(pl.multiple_of(y * 64, 64), 64)
    w_rows = pl.ds(pl.multiple_of(c * 256 + y * 64, 64), 64)

    def send_weights(k):
        for d in range(1, 4):
            to = plus(x, 4 - d)
            send(w_hbm.at[w_rows, columns(k, to)], wbuf.at[k, d, part],
                 wx_sem.at[0, k, d], wx_sem.at[1, k, d], at(x_=to))

    def weights(i, e):
        theirs = pl.ds(pl.multiple_of(plus(y, 4 - e) * 64, 64), 64)
        return wbuf.at[i // 2, pl.ds(1, 3), theirs, pl.ds(256 * (i % 2), 256)]

    met_x = set()

    def share_weights(i):
        if i // 2 not in met_x:
            met_x.add(i // 2)
            for d in range(1, 4):
                arrived(wbuf.at[i // 2, d, part], wx_sem.at[1, i // 2, d])
        piece = weights(i, 0)
        for e in (1, 3):
            send(piece, piece, wy_sem.at[0, i, e], wy_sem.at[1, i, e], at(y_=plus(y, e)))

    ahead = 1 + 2 * c

    def pass_weights(i):
        piece = weights(i, ahead)
        arrived(piece, wy_sem.at[1, i, ahead])
        send(piece, piece, wy_sem.at[0, i, 2], wy_sem.at[1, i, 2], at(y_=plus(y, ahead)))

    def await_weights(k):
        local_w[k].wait()
        for i in (2 * k, 2 * k + 1):
            for e in (4 - ahead, 2):
                arrived(weights(i, e), wy_sem.at[1, i, e])

    def pass_context(b):
        arrived(cbuf.at[4 - ahead, b], c_sem.at[1, b, 4 - ahead])
        send(cbuf.at[4 - ahead, b], cbuf.at[2, b], c_sem.at[0, b, 2], c_sem.at[1, b, 2],
             at(x_=plus(x, ahead)))

    def pass_pair(_):
        arrived(kvb.at[1 - mine, rows], kv_sem.at[1])
        send(kvb.at[1 - mine, rows], kvb.at[1 - mine, rows], kv_sem.at[2], kv_sem.at[3], at(1 - c))

    def await_pair(_):
        local_kv.wait()
        local_q.wait()
        other_rows = pl.ds(pl.multiple_of((1 - c) * HALF, HALF), HALF)
        arrived(kvb.at[1 - mine, other_rows], kv_sem.at[3])

    def send_key_weights(_):
        local_kw.wait()
        gain = jnp.broadcast_to(gain_ref[...], (8, COLS)).T[:, :1]
        gkb[z] = (kwb[...].astype(F32) * gain).astype(BF16).reshape(2, 256, KEYS)
        for e in range(1, 4):
            send(gkb.at[z, c, part], gkb.at[z, c, part], gs_sem.at[0, e], gr_sem.at[0, e],
                 at(z_=plus(z, e)))

    def key_weights(e_y):
        theirs = pl.ds(pl.multiple_of(plus(y, 4 - e_y) * 64, 64), 64)
        return [gkb.at[plus(z, e), c, theirs] for e in range(1, 4)]

    def share_key_weights(_):
        for e in range(1, 4):
            arrived(gkb.at[plus(z, 4 - e), c, part], gr_sem.at[0, e])
        for e_y in (1, 3):
            for i, piece in enumerate(key_weights(0)):
                send(piece, piece, gs_sem.at[e_y, i], gr_sem.at[e_y, i], at(y_=plus(y, e_y)))

    def pass_key_weights(_):
        for i, piece in enumerate(key_weights(ahead)):
            arrived(piece, gr_sem.at[ahead, i])
            send(piece, piece, gs_sem.at[2, i], gr_sem.at[2, i], at(y_=plus(y, ahead)))

    def swap_key_weights(_):
        for e_y in (4 - ahead, 2):
            for i, piece in enumerate(key_weights(e_y)):
                arrived(piece, gr_sem.at[e_y, i])
        for e in range(1, 4):
            piece = gkb.at[plus(z, e), c]
            send(piece, piece, gs_sem.at[4, e], gr_sem.at[4, e], at(1 - c))

    def await_key_weights():
        for e in range(1, 4):
            arrived(gkb.at[plus(z, e), 1 - c], gr_sem.at[4, e])

    def attend(index):
        seen = 128 * (index + 1)
        here = pl.ds(128 * index, 128)
        picked = jnp.concatenate([qbuf[here, :HEAD], qbuf[here, HEAD:]], axis=0)
        scores = dot(kvb[0, :seen, :], picked, ((1,), (1,)))
        first = seg_ref[:, here]
        first = jnp.concatenate([first, first], axis=1)
        key_at = lax.broadcasted_iota(jnp.int32, (seen, 256), 0)
        query_at = 128 * index + lax.broadcasted_iota(jnp.int32, (seen, 256), 1) % 128
        scores = jnp.where((key_at >= first) & (key_at <= query_at), scores, MASKED)
        top = jnp.max(scores, axis=0, keepdims=True)
        weights = jnp.exp2((scores - top) * SCALE)
        total = jnp.sum(weights, axis=0, keepdims=True)
        context = dot(kvb[1, :seen, :], weights.astype(BF16), ((0,), (0,)))
        return (context / total).T.astype(BF16)

    def context_block(b):
        for half in range(2):
            context = attend(b + 4 * half)
            there = pl.ds(128 * half, 128)
            cbuf[0, b, there, :HEAD] = context[:128]
            cbuf[0, b, there, HEAD:] = context[128:]
        for d in (1, 3):
            send(cbuf.at[0, b], cbuf.at[d, b], c_sem.at[0, b, d], c_sem.at[1, b, d],
                 at(x_=plus(x, 4 - d)))

    met_k, met_b = set(), set()

    def multiply(u):
        k, b = UNITS[u]
        if k not in met_k:
            met_k.add(k)
            await_weights(k)
        if b not in met_b:
            met_b.add(b)
            arrived(cbuf.at[ahead, b], c_sem.at[1, b, ahead])
            arrived(cbuf.at[2, b], c_sem.at[1, b, 2])
        total = dot(cbuf[0, b], wbuf[k, 0])
        for d in range(1, 4):
            total += dot(cbuf[d, b], wbuf[k, d])
        pbuf[u, 0] = total[:128]
        pbuf[u, 1] = total[128:]
        xsend[u] = pbuf[u, 1 - c].astype(BF16)
        send(xsend.at[u], xrecv.at[u], p_sem.at[0, u], p_sem.at[1, u], at(1 - c))

    def add_half(u):
        k, b = UNITS[u]
        arrived(xrecv.at[u], p_sem.at[1, u])
        total = pbuf[u, c] + xrecv[u].astype(F32)
        if k == 3:
            total += resb[pl.ds(128 * b, 128), :].astype(F32)
        pbuf[u, c] = total

    def pass_on(u):
        k, b = UNITS[u]
        to = owner[k]
        up = to > z
        has = (up & (z > 0)) | (jnp.logical_not(up) & (z < 3))

        @pl.when(has)
        def _():
            arrived(zrecv.at[to, b], zr_sem.at[to, b])
            zsend[k, b] = (pbuf[u, c] + zrecv[to, b].astype(F32)).astype(BF16)

        @pl.when(jnp.logical_not(has))
        def _():
            zsend[k, b] = pbuf[u, c].astype(BF16)

        following = jnp.where(up, z + 1, z - 1)
        slot = jnp.where(jnp.logical_not(up) & (to == following), 4, to)
        send(zsend.at[k, b], zrecv.at[slot, b], zs_sem.at[k, b], zr_sem.at[slot, b],
             at(z_=following))

    locals_ = []

    def hand(b):
        u = UNITS.index((3, b))
        held = pbuf.at[u, 1 - c]
        held[...] = pbuf[u, c]

        @pl.when(z > 0)
        def _():
            arrived(zrecv.at[z, b], zr_sem.at[z, b])
            held[...] += zrecv[z, b].astype(F32)

        @pl.when(z < 3)
        def _():
            arrived(zrecv.at[4, b], zr_sem.at[4, b])
            held[...] += zrecv[4, b].astype(F32)

        hbuf[b] = held[...].astype(BF16)
        place = pl.ds(pl.multiple_of(c * HALF + 128 * b, 128), 128)
        copy = pltpu.make_async_copy(hbuf.at[b], hand_hbm.at[place], hl_sem.at[b])
        copy.start()
        locals_.append(copy)
        send(hbuf.at[b], hand_hbm.at[place], h_sem.at[0, b], h_sem.at[1, b], at(1 - c))
        hidden = hbuf[b].astype(F32)
        sq1[b // 2, x, b % 2] = lax.dot_general(
            jnp.ones((8, COLS), F32), hidden * hidden, (((1,), (1,)), ((), ())),
            precision=lax.Precision.HIGHEST, preferred_element_type=F32,
        )

    met_key_weights = []

    def keys_1(g):
        if not met_key_weights:
            met_key_weights.append(g)
            await_key_weights()
        partial = jnp.zeros((GROUP, KEYS), F32)
        for k in range(4):
            u = UNITS.index((k, 2 * g))
            assert UNITS[u + 1] == (k, 2 * g + 1)
            held = jnp.concatenate([pbuf[u, c], pbuf[u + 1, c]], axis=0).astype(BF16)
            partial += dot(held, gkb[owner[k]].reshape(COLS, KEYS))
        k1s[g] = partial.astype(BF16)
        for d in range(1, 4):
            to = plus(x, 4 - d)
            send(k1s.at[g, pl.ds(pl.multiple_of(to * 64, 64), 64)], k1r.at[g, d],
                 ks_sem.at[0, g, d], kr_sem.at[0, g, d], at(x_=to))

    def keys_2(g):
        total = k1s[g, pl.ds(pl.multiple_of(x * 64, 64), 64), :].astype(F32)
        for d in range(1, 4):
            arrived(k1r.at[g, d], kr_sem.at[0, g, d])
            total += k1r[g, d].astype(F32)
        k2s[g] = total.astype(BF16)
        for e in range(1, 4):
            to = plus(z, e)
            send(k2s.at[g, pl.ds(pl.multiple_of(to * 16, 16), 16)], k2r.at[g, e],
                 ks_sem.at[1, g, e], kr_sem.at[1, g, e], at(z_=to))

    def keys_3(g):
        mine_ = pl.ds(pl.multiple_of(z * 16, 16), 16)
        total = k2s[g, mine_, :].astype(F32)
        for e in range(1, 4):
            arrived(k2r.at[g, e], kr_sem.at[1, g, e])
            total += k2r[g, e].astype(F32)
        place = pl.ds(pl.multiple_of(x * 64 + z * 16, 16), 16)
        k3[g, place, :] = total.astype(BF16)
        for e in range(1, 4):
            send(k3.at[g, place], k3.at[g, place], ks_sem.at[2, g, e], kr_sem.at[2, g, e],
                 at(z_=plus(z, e)))

    def keys_4(g):
        for e in range(1, 4):
            place = pl.ds(pl.multiple_of(x * 64 + plus(z, 4 - e) * 16, 16), 16)
            arrived(k3.at[g, place], kr_sem.at[2, g, e])
        held = k3.at[g, pl.ds(pl.multiple_of(x * 64, 64), 64)]
        place = keys_hbm.at[pl.ds(pl.multiple_of(GROUP * g + x * 64, 64), 64)]
        copy = pltpu.make_async_copy(held, place, kl_sem.at[g])
        copy.start()
        locals_.append(copy)
        for d in range(1, 4):
            send(held, place, ks_sem.at[3, g, d], kr_sem.at[3, g, d], at(x_=plus(x, d)))

    def squares_1(g):
        for d in range(1, 4):
            send(sq1.at[g, x], sq1.at[g, x], qs_sem.at[0, g, d], qr_sem.at[0, g, d],
                 at(x_=plus(x, d)))

    def squares_2(g):
        for d in range(1, 4):
            arrived(sq1.at[g, plus(x, 4 - d)], qr_sem.at[0, g, d])
        sq2[g, z] = (sq1[g, 0] + sq1[g, 1]) + (sq1[g, 2] + sq1[g, 3])
        for e in range(1, 4):
            send(sq2.at[g, z], sq2.at[g, z], qs_sem.at[1, g, e], qr_sem.at[1, g, e],
                 at(z_=plus(z, e)))

    def keys_5(g):
        for d in range(1, 4):
            place = pl.ds(pl.multiple_of(GROUP * g + plus(x, 4 - d) * 64, 64), 64)
            arrived(keys_hbm.at[place], kr_sem.at[3, g, d])
        for e in range(1, 4):
            arrived(sq2.at[g, plus(z, 4 - e)], qr_sem.at[1, g, e])
        squares_ref[g] = (sq2[g, 0] + sq2[g, 1]) + (sq2[g, 2] + sq2[g, 3])

    local_res.wait()
    send_weights(0)
    send_weights(1)
    send_weights(2)
    send_key_weights(0)
    share_weights(0)
    share_weights(1)
    pass_pair(0)
    await_pair(0)
    context_block(0)
    pass_weights(0)
    share_weights(2)
    share_weights(3)
    context_block(2)
    pass_context(0)
    pass_weights(1)
    share_weights(5)
    context_block(1)
    pass_context(2)
    share_weights(4)
    pass_weights(3)
    multiply(0)
    pass_weights(2)
    share_key_weights(0)
    add_half(0)
    pass_weights(5)
    pass_context(1)
    pass_on(0)
    send_weights(3)
    multiply(2)
    context_block(3)
    multiply(1)
    add_half(2)
    pass_on(2)
    multiply(4)
    multiply(6)
    pass_weights(4)
    multiply(5)
    share_weights(6)
    share_weights(7)
    add_half(1)
    pass_on(1)
    pass_key_weights(0)
    add_half(4)
    add_half(6)
    pass_context(3)
    pass_on(4)
    add_half(5)
    multiply(8)
    multiply(9)
    multiply(10)
    pass_on(6)
    pass_weights(6)
    add_half(8)
    multiply(11)
    multiply(3)
    add_half(10)
    multiply(7)
    pass_weights(7)
    add_half(9)
    add_half(11)
    add_half(3)
    pass_on(3)
    swap_key_weights(0)
    pass_on(5)
    pass_on(8)
    multiply(13)
    multiply(12)
    multiply(14)
    pass_on(9)
    multiply(15)
    add_half(13)
    add_half(12)
    keys_1(0)
    add_half(7)
    pass_on(10)
    add_half(14)
    add_half(15)
    keys_1(1)
    hand(0)
    keys_2(0)
    pass_on(7)
    hand(1)
    keys_2(1)
    squares_1(0)
    keys_3(0)
    pass_on(11)
    hand(2)
    keys_3(1)
    squares_2(0)
    keys_4(0)
    hand(3)
    squares_1(1)
    keys_4(1)
    keys_5(0)
    squares_2(1)
    keys_5(1)
    for b in range(4):
        place = pl.ds(pl.multiple_of((1 - c) * HALF + 128 * b, 128), 128)
        arrived(hand_hbm.at[place], h_sem.at[1, b])
    for copy in locals_:
        copy.wait()
    for copy in started:
        copy.wait_send()


def rotation():
    angles = np.arange(LEN)[:, None] * THETA ** (-2.0 * np.arange(HEAD // 2) / HEAD)[None, :]
    cosine, sine = np.cos(angles), np.sin(angles)
    return np.stack(
        [np.concatenate([cosine, cosine], 1), np.concatenate([-sine, sine], 1)]
    ).astype(np.float32)


def deliver(
    hand_in, keys_in, squares_hbm, bias_hbm, rot_hbm, hand_out, keys_out,
    hand, keys, out, rot, squares_ref, bias_ref, sem,
):
    rows = [pl.ds(256 * i, 256) for i in range(4)]
    half = pl.ds(pl.multiple_of(lax.axis_index("section") * HALF, HALF), HALF)
    first = [pltpu.make_async_copy(hand_in.at[r], hand.at[r], sem.at[0, i]) for i, r in enumerate(rows)]
    second = [pltpu.make_async_copy(hand.at[r], hand_out.at[r], sem.at[1, i]) for i, r in enumerate(rows)]
    keys_first = [pltpu.make_async_copy(keys_in.at[r], keys.at[r], sem.at[0, 4 + i]) for i, r in enumerate(rows[:2])]
    keys_second = [pltpu.make_async_copy(out.at[r], keys_out.at[r], sem.at[1, 4 + i]) for i, r in enumerate(rows[:2])]
    angles = pltpu.make_async_copy(rot_hbm.at[:, half], rot, sem.at[0, 6])
    small = [
        pltpu.make_async_copy(squares_hbm, squares_ref, sem.at[0, 7]),
        pltpu.make_async_copy(bias_hbm, bias_ref, sem.at[0, 8]),
    ]
    for copy in [*first, *small, *keys_first, angles]:
        copy.start()
    for arriving, leaving in zip(first, second, strict=True):
        arriving.wait()
        leaving.start()
    for copy in small:
        copy.wait()
    inverse = lax.rsqrt(squares_ref[...] / D + EPS)
    angles.wait()
    for g in range(2):
        keys_first[g].wait()
        for i in range(2):
            at_rows = pl.ds(GROUP * g + 128 * i, 128)
            projected = keys[at_rows, :].astype(F32) * inverse[g, i].T[:, :1] + bias_ref[...]
            cosine, sine = rot[0, at_rows, :], rot[1, at_rows, :]
            for head in range(KEYS // HEAD):
                v = projected[:, head * HEAD : (head + 1) * HEAD]
                crossed = jnp.concatenate([v[:, HEAD // 2 :], v[:, : HEAD // 2]], axis=1)
                out[at_rows, pl.ds(head * HEAD, HEAD)] = (v * cosine + crossed * sine).astype(BF16)
        keys_second[g].start()
    for copy in second + keys_second:
        copy.wait()


def local(queries, keys_values, segments, residual, out_weight, key_weight, key_bias, norm_gain):
    hbm = pl.BlockSpec(memory_space=pl.ANY)
    vmem = pl.BlockSpec(memory_space=pltpu.VMEM)
    dma = pltpu.SemaphoreType.DMA
    handed, keys, squares = pl.pallas_call(
        kernel,
        out_shape=(
            jax.ShapeDtypeStruct((LEN, COLS), BF16),
            jax.ShapeDtypeStruct((HALF, KEYS), BF16),
            jax.ShapeDtypeStruct((2, 2, 8, 128), F32),
        ),
        in_specs=[hbm, hbm, vmem, hbm, hbm, hbm, vmem],
        out_specs=(hbm, hbm, vmem),
        scratch_shapes=[
            pltpu.VMEM((LEN, 256), BF16),
            pltpu.VMEM((2, LEN, HEAD), BF16),
            pltpu.VMEM((4, 4, 256, COLS), BF16),
            pltpu.VMEM((HALF, COLS), BF16),
            pltpu.VMEM((COLS, KEYS), BF16),
            pltpu.VMEM((4, 2, 256, KEYS), BF16),
            pltpu.VMEM((4, 4, 256, 256), BF16),
            pltpu.VMEM((16, 2, 128, COLS), F32),
            pltpu.VMEM((16, 128, COLS), BF16),
            pltpu.VMEM((16, 128, COLS), BF16),
            pltpu.VMEM((3, 4, 128, COLS), BF16),
            pltpu.VMEM((5, 4, 128, COLS), BF16),
            pltpu.VMEM((4, 128, COLS), BF16),
            pltpu.VMEM((2, GROUP, KEYS), BF16),
            pltpu.VMEM((2, 4, 64, KEYS), BF16),
            pltpu.VMEM((2, 64, KEYS), BF16),
            pltpu.VMEM((2, 4, 16, KEYS), BF16),
            pltpu.VMEM((2, GROUP, KEYS), BF16),
            pltpu.VMEM((2, 4, 2, 8, 128), F32),
            pltpu.VMEM((2, 4, 2, 8, 128), F32),
            dma((6,)),
            dma((4,)),
            dma((4,)),
            dma((2, 4, 4)),
            dma((2, 8, 4)),
            dma((2, 4, 4)),
            dma((2, 16)),
            dma((3, 4)),
            dma((5, 4)),
            dma((2, 4)),
            dma((4,)),
            dma((5, 4)),
            dma((5, 4)),
            dma((4, 2, 4)),
            dma((4, 2, 4)),
            dma((2,)),
            dma((2, 2, 4)),
            dma((2, 2, 4)),
        ],
        compiler_params=pltpu.CompilerParams(
            collective_id=0, has_side_effects=True, vmem_limit_bytes=56 << 20
        ),
        name="relay",
    )(
        queries[0], keys_values[0], segments, residual[0], out_weight, key_weight,
        norm_gain.reshape(1, COLS),
    )
    handed, keys = pl.pallas_call(
        deliver,
        out_shape=(
            jax.ShapeDtypeStruct((LEN, COLS), BF16),
            jax.ShapeDtypeStruct((HALF, KEYS), BF16),
        ),
        in_specs=[hbm, hbm, hbm, hbm, hbm],
        out_specs=(hbm, hbm),
        scratch_shapes=[
            pltpu.VMEM((LEN, COLS), BF16),
            pltpu.VMEM((HALF, KEYS), BF16),
            pltpu.VMEM((HALF, KEYS), BF16),
            pltpu.VMEM((2, HALF, HEAD), F32),
            pltpu.VMEM((2, 2, 8, 128), F32),
            pltpu.VMEM((1, KEYS), F32),
            dma((2, 9)),
        ],
        compiler_params=pltpu.CompilerParams(vmem_limit_bytes=60 << 20),
        name="deliver",
    )(handed, keys, squares, key_bias.reshape(1, KEYS), jnp.asarray(rotation()))
    return handed[None], keys[None]


def solution(mesh):
    return jax.shard_map(
        local,
        mesh=mesh,
        in_specs=(
            P("narrow", None, "wide"),
            P("narrow", None, "wide"),
            P("narrow", None),
            P("narrow", None, "wide"),
            P("wide", None),
            P("wide", None),
            P(),
            P("wide"),
        ),
        out_specs=(P("narrow", None, "wide"), P("narrow", "section", None)),
        check_vma=False,
    )
```
